32 devices in a mesh: shard: 4 (over z), ctx: 4 (over x, core), tp: 2 (over y).
Axes of the slice: x: 2, y: 2, z: 4, core: 2. Of those that a mesh axis runs over, the one named last changes fastest.
Arguments:
- frames: bfloat16 [2, 4, 2048, 1280], P(None, 'shard', 'ctx'), may hold values from -6 to 6
- lengths: int32 [2, 4], P(None, 'shard'), may hold values from 256 to 2048, as said below
- norm1_gain: float32 [1280], replicated, may hold values from 0.1 to 1.9
- norm1_bias: float32 [1280], replicated, may hold values from -1.8 to 1.8
- query_weight: bfloat16 [1280, 1280], P('shard', 'tp'), may hold values from -0.15625 to 0.15625
- query_bias: float32 [1280], P('tp'), may hold values from -3 to 3
- key_weight: bfloat16 [1280, 1280], P('shard', 'tp'), may hold values from -0.15625 to 0.15625
- value_weight: bfloat16 [1280, 1280], P('shard', 'tp'), may hold values from -0.15625 to 0.15625
- value_bias: float32 [1280], P('tp'), may hold values from -1.2 to 1.2
- out_weight: bfloat16 [1280, 1280], P('shard', 'tp'), may hold values from -0.625 to 0.625
- out_bias: float32 [1280], replicated, may hold values from -1.8 to 1.8
- norm2_gain: float32 [1280], replicated, may hold values from 0.1 to 1.9
- norm2_bias: float32 [1280], replicated, may hold values from -1.8 to 1.8
- up_weight: bfloat16 [1280, 5120], P('shard', 'tp'), may hold values from -0.15625 to 0.15625
- up_bias: float32 [5120], P('tp'), may hold values from -1.8 to 1.8
- down_weight: bfloat16 [1280, 5120], P('shard', 'tp'), may hold values from -0.125 to 0.125
- down_bias: float32 [1280], replicated, may hold values from -1.8 to 1.8
- cotangent: bfloat16 [2, 4, 2048, 1280], P(None, 'shard', 'ctx'), may hold values from -6 to 6
Outputs:
- output: bfloat16 [2, 4, 2048, 1280], P(None, 'shard', 'ctx')
- frames_grad: float32 [2, 4, 2048, 1280], P(None, 'shard', 'ctx')
- norm1_gain_grad: float32 [1280], replicated
- norm1_bias_grad: float32 [1280], replicated
- query_weight_grad: float32 [1280, 1280], P('shard', 'tp')
- query_bias_grad: float32 [1280], P('tp')
- key_weight_grad: float32 [1280, 1280], P('shard', 'tp')
- value_weight_grad: float32 [1280, 1280], P('shard', 'tp')
- value_bias_grad: float32 [1280], P('tp')
- out_weight_grad: float32 [1280, 1280], P('shard', 'tp')
- out_bias_grad: float32 [1280], replicated
- norm2_gain_grad: float32 [1280], replicated
- norm2_bias_grad: float32 [1280], replicated
- up_weight_grad: float32 [1280, 5120], P('shard', 'tp')
- up_bias_grad: float32 [5120], P('tp')
- down_weight_grad: float32 [1280, 5120], P('shard', 'tp')
- down_bias_grad: float32 [1280], replicated
The draws below stay inside these ranges and needn't reach their ends.
Inputs may be any that keep to these rules, and one draw needn't show every extreme that they name: Each clip's number of valid frames lies between the stated bounds; of the 2 clips lengths[:, b] that share a column b, one has exactly 2048.
All inputs are finite; a program needn't handle non-finite values.
Results may differ from the reference program's by a relative error of at most 0.02.
Values may be sent and summed in bfloat16 or wider, within the bound.
A program may use at most 224 MiB of HBM per device.

```python
import jax
import jax.numpy as jnp
from jax import lax

D = 1280
HEADS = 16
HEAD_DIM = 80
FF = 5120
MICRO = 2
BATCH = 4
LENGTH = 2048


def draw_lengths(key, part):
    key = jax.random.fold_in(key, 11)
    key_draw, key_full = jax.random.split(key)
    lowest = max(1, LENGTH // 8)
    drawn_lengths = jax.random.randint(key_draw, (MICRO, BATCH), lowest, LENGTH + 1)
    full_row = jax.random.randint(key_full, (1, BATCH), 0, MICRO)
    row_index = jnp.arange(MICRO, dtype=jnp.int32)[:, None]
    return jnp.where(row_index == full_row, LENGTH, drawn_lengths).astype(jnp.int32)


def steps_of(key, extent, shards, smallest, high):
    def one(position, shards_of):
        heights = jax.random.uniform(jax.random.fold_in(jax.random.fold_in(key, 6), position), (shards_of,), jnp.float32, smallest / len(shards), high / len(shards))
        return jnp.repeat(jnp.exp(heights), extent[position] // shards_of).reshape((-1,) + (1,) * (len(extent) - position - 1))

    level = one(*shards[0])
    for cut in shards[1:]:
        level = level * one(*cut)
    return level


def bell_draw(key, extent, scale, most, cuts=(), kind=jnp.bfloat16):
    array = jax.random.normal(key, extent, jnp.float32) * scale
    if len(cuts) > 0:
        array = steps_of(key, extent, cuts, -0.22, 0.18) * array
    return jnp.clip(array, min=-most, max=most).astype(kind)


def setup_inputs(seed: int = 0) -> dict:
    key_of = jax.random.split(jax.random.key(seed), 19)
    return {
        "frames": bell_draw(key_of[0], (MICRO, BATCH, LENGTH, D), 1.0, 6.0, ((1, 4), (2, 4))),
        "lengths": draw_lengths(jax.random.fold_in(key_of[18], 71), 0),
        "norm1_gain": jnp.clip(1.0 + 0.18 * jax.random.normal(key_of[2], (D,), jnp.float32), 0.1, 1.9),
        "norm1_bias": bell_draw(key_of[3], (D,), 0.3, 1.8, (), jnp.float32),
        "query_weight": bell_draw(key_of[4], (D, D), D ** -0.5, 0.15625, ((0, 4), (1, 2))),
        "query_bias": bell_draw(key_of[5], (D,), 0.5, 3.0, ((0, 2),), jnp.float32),
        "key_weight": bell_draw(key_of[6], (D, D), D ** -0.5, 0.15625, ((0, 4), (1, 2))),
        "value_weight": bell_draw(key_of[7], (D, D), D ** -0.5, 0.15625, ((0, 4), (1, 2))),
        "value_bias": bell_draw(key_of[8], (D,), 0.2, 1.2, ((0, 2),), jnp.float32),
        "out_weight": bell_draw(key_of[9], (D, D), (D // 16) ** -0.5, 0.625, ((0, 4), (1, 2))),
        "out_bias": bell_draw(key_of[10], (D,), 0.3, 1.8, (), jnp.float32),
        "norm2_gain": jnp.clip(1.0 + 0.18 * jax.random.normal(key_of[11], (D,), jnp.float32), 0.1, 1.9),
        "norm2_bias": bell_draw(key_of[12], (D,), 0.3, 1.8, (), jnp.float32),
        "up_weight": bell_draw(key_of[13], (D, FF), D ** -0.5, 0.15625, ((0, 4), (1, 2))),
        "up_bias": bell_draw(key_of[14], (FF,), 0.3, 1.8, ((0, 2),), jnp.float32),
        "down_weight": bell_draw(key_of[15], (D, FF), (FF // 2) ** -0.5, 0.125, ((0, 4), (1, 2))),
        "down_bias": bell_draw(key_of[16], (D,), 0.3, 1.8, (), jnp.float32),
        "cotangent": bell_draw(key_of[17], (MICRO, BATCH, LENGTH, D), 1.0, 6.0, ((1, 4), (2, 4))),
    }


@jax.custom_vjp
def low(v):
    return lax.optimization_barrier(v.astype(jnp.bfloat16)).astype(jnp.float32)

@jax.custom_vjp
def low_back(v):
    return v

def low_keep(v):
    return (low(v), None)

def low_pass(kept, grad):
    return (grad,)

def back_keep(v):
    return (v, None)

def back_low(kept, grad):
    return (low(grad),)
low.defvjp(low_keep, low_pass)
low_back.defvjp(back_keep, back_low)
epsilon = 1e-05

def layer_norm(values, gain, bias):
    center = values - lax.optimization_barrier(jnp.mean(values, axis=-1, keepdims=True))
    spread = lax.optimization_barrier(jnp.mean(center * center, axis=-1, keepdims=True))
    return center * lax.rsqrt(spread + epsilon) * gain + bias

def exact_gelu(values):
    return jax.nn.gelu(values, approximate=False)

def matmul(left, right):
    return jnp.dot(left, right, precision=lax.Precision.HIGHEST, preferred_element_type=jnp.float32)

def clip_layer(params, clip_rows, length):
    norm1_gain, norm1_bias, query_weight, query_bias, key_weight, value_weight, value_bias, out_weight, out_bias, norm2_gain, norm2_bias, up_weight, up_bias, down_weight, down_bias = params
    normed = low(layer_norm(clip_rows, norm1_gain, norm1_bias))
    queries = low(low_back(matmul(normed, query_weight) + query_bias))
    keys = low(low_back(matmul(normed, key_weight)))
    values = low(low_back(matmul(normed, value_weight) + value_bias))
    query_heads = queries.reshape(LENGTH, HEADS, HEAD_DIM)
    key_heads = keys.reshape(LENGTH, HEADS, HEAD_DIM)
    value_heads = values.reshape(LENGTH, HEADS, HEAD_DIM)
    scores = jnp.einsum('qhd,khd->hqk', query_heads, key_heads, precision=lax.Precision.HIGHEST) * HEAD_DIM ** (-0.5)
    key_valid = jnp.arange(LENGTH, dtype=jnp.int32) < length
    scores = low_back(jnp.where(key_valid[None, None, :], scores, -1000000000.0))
    attn_probs = low(jax.nn.softmax(scores, axis=-1))
    attended = jnp.einsum('hqk,khd->qhd', attn_probs, value_heads, precision=lax.Precision.HIGHEST)
    attended = low(low_back(attended.reshape(LENGTH, D)))
    branch = low_back(matmul(attended, out_weight.T))
    mixed = clip_rows + branch + out_bias
    normed2 = low(layer_norm(mixed, norm2_gain, norm2_bias))
    hidden = low_back(matmul(normed2, up_weight) + up_bias)
    activated = low(exact_gelu(hidden))
    return mixed + matmul(activated, down_weight.T) + down_bias

def reference(frames, lengths, norm1_gain, norm1_bias, query_weight, query_bias, key_weight, value_weight, value_bias, out_weight, out_bias, norm2_gain, norm2_bias, up_weight, up_bias, down_weight, down_bias, cotangent):
    params = tuple((item.astype(jnp.float32) for item in (norm1_gain, norm1_bias, query_weight, query_bias, key_weight, value_weight, value_bias, out_weight, out_bias, norm2_gain, norm2_bias, up_weight, up_bias, down_weight, down_bias)))
    inputs = frames.astype(jnp.float32)
    flat_lengths = lengths.reshape(MICRO * BATCH).astype(jnp.int32)

    def forward(layer_input, weights):
        flat_rows = layer_input.reshape(MICRO * BATCH, LENGTH, D)

        def one_clip(packed):
            return clip_layer(weights, packed[0], packed[1])
        done = lax.map(jax.checkpoint(one_clip), (flat_rows, flat_lengths))
        return done.reshape(MICRO, BATCH, LENGTH, D)
    result, pullback = jax.vjp(forward, inputs, params)
    frames_grad, grads = pullback(cotangent.astype(jnp.float32))
    return (result.astype(jnp.bfloat16), frames_grad, grads[0], grads[1], grads[2], grads[3], grads[4], grads[5], grads[6], grads[7], grads[8], grads[9], grads[10], grads[11], grads[12], grads[13], grads[14])
```

```python
import functools
import math

import jax
import jax.numpy as jnp
from jax import lax
from jax.experimental import pallas as pl
from jax.experimental.pallas import tpu as pltpu
from jax.sharding import PartitionSpec as P

HEAD_DIM = 80
STEP = 512
SUB = 256
EPSILON = 1e-05
SCALE = HEAD_DIM**-0.5
LOW = jnp.bfloat16


def contract(left, right, dims):
    return lax.dot_general(left, right, (dims, ((), ())), preferred_element_type=jnp.float32)

def forward_kernel(valid_ref, q_ref, *refs, blocks, heads):
    k_refs, v_refs = refs[:blocks], refs[blocks:2*blocks]
    a_ref, e_ref, inverse_ref, s0_ref, s1_ref, m0_ref, m1_ref, acc_ref, l_ref = refs[2*blocks:]
    h = pl.program_id(0)
    q = q_ref[...]
    span = k_refs[0].shape[1]
    acc_ref[...] = jnp.zeros(acc_ref.shape, jnp.float32)
    l_ref[...] = jnp.zeros(l_ref.shape, jnp.float32)
    step=min(STEP,span)
    def go(s_now, m_now, s_before, m_before):
        m_now[...] = jnp.full(m_now.shape, -1e30, jnp.float32)
        m_last = m_before[...]
        for b in range(blocks):
            for off in range(0, span, step):
                left = valid_ref[b] - off
                def work():
                    rows = slice(b*span+off, b*span+off+step)
                    s = contract(k_refs[b][:, off:off+step], q, ((0,), (0,)))
                    e = jnp.exp2(s_before[rows] - m_last)
                    row = lax.broadcasted_iota(jnp.int32, (step, 1), 0)
                    s = jnp.where(row < left, s, -1e30)
                    s_now[rows] = s
                    m_now[...] = jnp.maximum(m_now[...], jnp.max(s, axis=0, keepdims=True))
                    l_ref[...] += jnp.sum(e, axis=0, keepdims=True)
                    low = e.astype(jnp.bfloat16)
                    e_ref[0, rows] = low
                    acc_ref[...] += contract(v_refs[b][:, off:off+step], low, ((1,), (0,)))
                work()
    @pl.when(lax.rem(h, 2) == 0)
    def _():
        go(s0_ref, m0_ref, s1_ref, m1_ref)
    @pl.when(lax.rem(h, 2) == 1)
    def _():
        go(s1_ref, m1_ref, s0_ref, m0_ref)
    inverse = 1.0 / l_ref[...]
    a_ref[...] = (acc_ref[...] * inverse).astype(jnp.bfloat16)
    inverse_ref[0] = jnp.broadcast_to(inverse, inverse_ref.shape[1:])

def attention_forward(valid, q, kv):
    width, rows = q.shape
    heads = width // HEAD_DIM
    blocks, span = len(kv), kv[0].shape[1]
    head = lambda h: (jnp.minimum(h, heads-1), 0)
    last = lambda h: (jnp.maximum(h-1, 0), 0)
    value = lambda h: (heads + jnp.maximum(h-1, 0), 0)
    return pl.pallas_call(
        functools.partial(forward_kernel, blocks=blocks, heads=heads),
        grid=(heads+1,),
        in_specs=[pl.BlockSpec(memory_space=pltpu.SMEM), pl.BlockSpec((HEAD_DIM, rows), head)]
          + [pl.BlockSpec((HEAD_DIM, span), head)]*blocks + [pl.BlockSpec((HEAD_DIM, span), value)]*blocks,
        out_specs=[pl.BlockSpec((HEAD_DIM, rows), last), pl.BlockSpec((1, blocks*span, rows), lambda h:(jnp.maximum(h-1,0),0,0)), pl.BlockSpec((1,8,rows), lambda h:(jnp.maximum(h-1,0),0,0))],
        out_shape=[jax.ShapeDtypeStruct((width, rows), jnp.bfloat16), jax.ShapeDtypeStruct((heads, blocks*span, rows), jnp.bfloat16), jax.ShapeDtypeStruct((heads, 8, rows), jnp.float32)],
        scratch_shapes=[pltpu.VMEM((blocks*span, rows), jnp.float32), pltpu.VMEM((blocks*span, rows), jnp.float32), pltpu.VMEM((1, rows), jnp.float32), pltpu.VMEM((1, rows), jnp.float32), pltpu.VMEM((HEAD_DIM, rows), jnp.float32), pltpu.VMEM((1, rows), jnp.float32)],
        compiler_params=pltpu.CompilerParams(vmem_limit_bytes=40<<20),
        cost_estimate=pl.CostEstimate(flops=4*rows*blocks*span*256*heads, bytes_accessed=heads*blocks*span*rows*2, transcendentals=rows*blocks*span*heads),
        name="attention_forward",
    )(valid, q, *kv, *kv)

def backward_kernel(valid_ref, q_ref, g_ref, a_ref, inverse_ref, e_ref, *refs, blocks):
    k_refs, v_refs = refs[:blocks], refs[blocks:2*blocks]
    dq_ref = refs[2*blocks]
    dk_refs, dv_refs = refs[2*blocks+1:3*blocks+1], refs[3*blocks+1:4*blocks+1]
    acc_ref = refs[4*blocks+1]
    q = q_ref[...]
    g32 = g_ref[...].astype(jnp.float32) * inverse_ref[0, 0:1]
    delta = jnp.sum(g32 * a_ref[...].astype(jnp.float32), axis=0, keepdims=True)
    g = g32.astype(jnp.bfloat16)
    span = k_refs[0].shape[1]
    step=min(STEP,span)
    acc_ref[...] = jnp.zeros(acc_ref.shape, jnp.float32)
    for b in range(blocks):
        for off in range(0, span, step):
            left = valid_ref[b] - off
            cols = slice(off, off+step)
            rows = slice(b*span+off, b*span+off+step)
            def work():
                sub = min(SUB, step)
                parts = [(slice(off+o, off+o+sub), slice(b*span+off+o, b*span+off+o+sub)) for o in range(0, step, sub)]
                dps = [contract(v_refs[b][:, c], g, ((0,), (0,))) for c, r in parts]
                total = None
                for (c, r), dp in zip(parts, dps):
                    e = e_ref[0, r]
                    dv_refs[b][:, c] = contract(g, e, ((1,), (1,))).astype(jnp.bfloat16)
                    ds = (e.astype(jnp.float32) * (dp - delta)).astype(jnp.bfloat16)
                    t = contract(k_refs[b][:, c], ds, ((1,), (0,)))
                    total = t if total is None else total + t
                    dk_refs[b][:, c] = (contract(q, ds, ((1,), (1,))) * math.log(2.0)).astype(jnp.bfloat16)
                acc_ref[...] += total
            work()
    dq_ref[...] = (acc_ref[...] * HEAD_DIM**-0.5).astype(jnp.bfloat16)

def attention_backward(valid, q, g, a, inverse, e, kv):
    width, rows = q.shape
    heads = width // HEAD_DIM
    blocks, span = len(kv), kv[0].shape[1]
    head = lambda h: (h, 0)
    value = lambda h: (heads + h, 0)
    hspec = pl.BlockSpec((HEAD_DIM, rows), head)
    kspec = pl.BlockSpec((HEAD_DIM, span), head)
    vspec = pl.BlockSpec((HEAD_DIM, span), value)
    out = jax.ShapeDtypeStruct((width, span), jnp.bfloat16)
    return pl.pallas_call(
        functools.partial(backward_kernel, blocks=blocks),
        grid=(heads,),
        in_specs=[pl.BlockSpec(memory_space=pltpu.SMEM), hspec, hspec, hspec, pl.BlockSpec((1,8,rows), lambda h:(h,0,0)), pl.BlockSpec((1, blocks*span, rows), lambda h:(h,0,0))]
          + [kspec]*blocks + [vspec]*blocks,
        out_specs=[hspec] + [kspec]*(2*blocks),
        out_shape=[jax.ShapeDtypeStruct((width, rows), jnp.bfloat16)] + [out]*(2*blocks),
        scratch_shapes=[pltpu.VMEM((HEAD_DIM, rows), jnp.float32)],
        compiler_params=pltpu.CompilerParams(vmem_limit_bytes=40<<20),
        cost_estimate=pl.CostEstimate(flops=8*rows*blocks*span*256*heads, bytes_accessed=heads*blocks*span*rows*2, transcendentals=0),
        name="attention_backward",
    )(valid, q, g, a, inverse, e, *kv, *kv)


def swap(value, axis, bit, size):
    return lax.ppermute(value, axis, [(k, k ^ bit) for k in range(size)])


def bits_of(size):
    found, bit = [], size // 2
    while bit > 0:
        found.append(bit)
        bit //= 2
    return found


def spread(value, axis, size):
    blocks = {0: value}
    for bit in bits_of(size):
        blocks.update({mask | bit: swap(blocks[mask], axis, bit, size) for mask in list(blocks)})
    return [blocks[mask] for mask in range(size)]


def pair_sum(value, axis, size):
    for bit in reversed(bits_of(size)):
        value = value + swap(value, axis, bit, size)
    return value


def low_sum(value, axis, size):
    if size == 1:
        return value
    total = value.astype(LOW)
    for bit in reversed(bits_of(size)):
        total = (total.astype(jnp.float32) + swap(total, axis, bit, size).astype(jnp.float32)).astype(LOW)
    return total.astype(jnp.float32)


def canonical(blocks, axis, size):
    me = lax.axis_index(axis)
    out = jnp.zeros((size,) + blocks[0].shape, blocks[0].dtype)
    for mask, block in enumerate(blocks):
        out = lax.dynamic_update_index_in_dim(out, block, me ^ mask, 0)
    return out


def gather_rows(piece, size):
    me = lax.axis_index("shard")
    right, left = [piece], [piece]
    for hop in range(1, size):
        right.append(lax.ppermute(right[-1], "shard", [(k, k + 1) for k in range(hop - 1, size - 1)]))
        left.append(lax.ppermute(left[-1], "shard", [(k, k - 1) for k in range(size - hop, 0, -1)]))
    out = jnp.zeros((size,) + piece.shape, piece.dtype)
    out = lax.dynamic_update_index_in_dim(out, piece, me, 0)
    for hop in range(1, size):
        block = jnp.where(me >= hop, right[hop], left[size - hop])
        out = lax.dynamic_update_index_in_dim(out, block, lax.rem(me + size - hop, size), 0)
    return out


def gather_weight(weight, shard, ctx, split):
    part = lax.rem(lax.axis_index("ctx"), split)
    rows = weight.shape[0] // split
    piece = lax.dynamic_slice_in_dim(weight, part * rows, rows, 0)
    mine = gather_rows(piece, shard)
    blocks = {0: mine}
    for bit in bits_of(split):
        blocks.update({mask | bit: swap(blocks[mask], "ctx", bit, ctx) for mask in list(blocks)})
    out = jnp.zeros((shard, split, rows, weight.shape[1]), weight.dtype)
    for mask in range(split):
        out = lax.dynamic_update_index_in_dim(out, blocks[mask], part ^ mask, 1)
    return out.reshape(shard * weight.shape[0], weight.shape[1])


def scatter_ctx(chunk, ctx):
    def total(mask, bits):
        if len(bits) == 0:
            return chunk(mask)
        bit, rest = bits[0], bits[1:]
        away = total(mask | bit, rest).astype(LOW)
        return total(mask, rest) + swap(away, "ctx", bit, ctx).astype(jnp.float32)

    return total(0, bits_of(ctx))


def scatter_rows(full, size):
    me = lax.axis_index("shard")
    rows = full.shape[0] // size
    total = lax.dynamic_slice_in_dim(full, me * rows, rows, 0)
    low = full.astype(LOW)
    for shift in range(1, size):
        there = lax.rem(me + shift, size)
        block = lax.dynamic_slice_in_dim(low, there * rows, rows, 0)
        got = lax.ppermute(block, "shard", [(k, (k + shift) % size) for k in range(size)])
        total = total + got.astype(jnp.float32)
    return total


def weight_grad(left, right, right_dim, shard, ctx):
    count = right.shape[right_dim] // ctx
    me = lax.axis_index("ctx")

    def chunk(mask):
        part = lax.dynamic_slice_in_dim(right, (me ^ mask) * count, count, right_dim)
        return contract(left, part, ((0,), (1 - right_dim,)))

    mine = scatter_rows(scatter_ctx(chunk, ctx), shard).astype(LOW)
    blocks = canonical(spread(mine, "ctx", ctx), "ctx", ctx)
    return jnp.moveaxis(blocks, 0, 1).reshape(mine.shape[0], ctx * count).astype(jnp.float32)


def normalize(values):
    center = values - jnp.mean(values, axis=-1, keepdims=True)
    spread_of = jnp.mean(center * center, axis=-1, keepdims=True)
    inverse = lax.rsqrt(spread_of + EPSILON)
    return center * inverse, inverse


def normalize_grad(grad, hat, inverse):
    return inverse * (
        grad - jnp.mean(grad, axis=-1, keepdims=True) - hat * jnp.mean(grad * hat, axis=-1, keepdims=True)
    )


def body(
    sizes,
    frames,
    lengths,
    norm1_gain,
    norm1_bias,
    query_weight,
    query_bias,
    key_weight,
    value_weight,
    value_bias,
    out_weight,
    out_bias,
    norm2_gain,
    norm2_bias,
    up_weight,
    up_bias,
    down_weight,
    down_bias,
    cotangent,
):
    shard, ctx, tp = sizes
    micros, rows = frames.shape[0], frames.shape[2]
    width = query_weight.shape[1]
    ctx_index = lax.axis_index("ctx")

    full_qkv = gather_weight(
        jnp.concatenate([query_weight, key_weight, value_weight], axis=1), shard, ctx, 4 if ctx % 4 == 0 else 1
    )
    out_both = canonical(spread(out_weight, "tp", tp), "tp", tp)
    out_both = jnp.moveaxis(out_both, 0, 1).reshape(out_weight.shape[0], tp * width)
    full_out = gather_weight(out_both, shard, ctx, 2)
    full_up = gather_weight(up_weight, shard, ctx, 4)
    full_down = gather_weight(down_weight, shard, ctx, 2)
    own_out = lax.dynamic_slice_in_dim(full_out, lax.axis_index("tp") * width, width, 1)

    bias = jnp.concatenate([query_bias, jnp.zeros_like(query_bias), value_bias])[:, None]
    scale = jnp.concatenate(
        [jnp.full((width, 1), SCALE * math.log2(math.e), jnp.float32), jnp.ones((2 * width, 1), jnp.float32)]
    )

    inputs = [frames[m, 0].astype(jnp.float32) for m in range(micros)]
    hats1 = [normalize(x) for x in inputs]
    normed1 = [(hat * norm1_gain + norm1_bias).astype(LOW) for hat, _ in hats1]
    projected = [((contract(full_qkv, h, ((0,), (1,))) + bias) * scale).astype(LOW) for h in normed1]
    queries = [p[:width] for p in projected]
    pairs = [spread(p[width:], "ctx", ctx) for p in projected]
    ids = ctx_index ^ jnp.arange(ctx, dtype=jnp.int32)
    valid = [jnp.clip(lengths[m, 0] - rows * ids, 0, rows) for m in range(micros)]

    attended, kept, inverses = zip(*[attention_forward(valid[m], queries[m], pairs[m]) for m in range(micros)])
    mixed, hats2, normed2, hidden = [], [], [], []
    for m in range(micros):
        all_heads = canonical(spread(attended[m], "tp", tp), "tp", tp).reshape(tp * width, rows)
        mixed.append(inputs[m] + contract(all_heads, full_out, ((0,), (1,))) + out_bias)
        hats2.append(normalize(mixed[m]))
        normed2.append((hats2[m][0] * norm2_gain + norm2_bias).astype(LOW))
        hidden.append(contract(normed2[m], full_up, ((1,), (0,))) + up_bias)
    active, hidden_grads, outputs, mixed_grads, branch_grads = [], [], [], [], []
    normed2_grads = []
    for m in range(micros):
        cdf = 0.5 * (1.0 + lax.erf(hidden[m] * math.sqrt(0.5)))
        pdf = jnp.exp(-0.5 * hidden[m] * hidden[m]) * (1.0 / math.sqrt(2.0 * math.pi))
        active.append((hidden[m] * cdf).astype(LOW))
        slope = cdf + hidden[m] * pdf
        hidden_grads.append((contract(cotangent[m, 0], full_down, ((1,), (0,))) * slope).astype(LOW))
        normed2_grads.append(low_sum(contract(hidden_grads[m], full_up, ((1,), (1,))), "tp", tp))
    for m in range(micros):
        branch = low_sum(contract(active[m], full_down, ((1,), (1,))), "tp", tp)
        outputs.append((mixed[m] + branch + down_bias).astype(LOW))
        hat, inverse = hats2[m]
        mixed_grads.append(
            cotangent[m, 0].astype(jnp.float32) + normalize_grad(normed2_grads[m] * norm2_gain, hat, inverse)
        )
        branch_grads.append(mixed_grads[m].astype(LOW))
    projected_grads, normed1_terms, input_grads = [], [], []
    for m in range(micros):
        attended_grad = contract(own_out, branch_grads[m], ((0,), (1,))).astype(LOW)
        parts = attention_backward(
            valid[m], queries[m], attended_grad, attended[m], inverses[m], kept[m], pairs[m]
        )
        terms = [
            jnp.concatenate([parts[1 + mask], parts[1 + ctx + mask]], axis=0) for mask in range(ctx)
        ]
        pair_grad = scatter_ctx(lambda mask: terms[mask].astype(jnp.float32), ctx).astype(LOW)
        projected_grads.append(jnp.concatenate([parts[0], pair_grad], axis=0))
        normed1_terms.append(contract(projected_grads[m], full_qkv, ((0,), (1,))))
    gain1, bias1 = [], []
    for m in range(micros):
        hat, inverse = hats1[m]
        gain1.append(jnp.sum(normed1_terms[m] * hat, axis=0))
        bias1.append(jnp.sum(normed1_terms[m], axis=0))
        total = low_sum(normed1_terms[m], "tp", tp)
        input_grads.append(mixed_grads[m] + normalize_grad(total * norm1_gain, hat, inverse))

    def over(items, dim):
        return jnp.concatenate(items, axis=dim)

    up_grad = weight_grad(over(normed2, 0), over(hidden_grads, 0), 1, shard, ctx)
    down_grad = weight_grad(over([cotangent[m, 0] for m in range(micros)], 0), over(active, 0), 1, shard, ctx)
    out_grad = weight_grad(over(branch_grads, 0), over(attended, 1), 0, shard, ctx)
    projected_all = over(projected_grads, 1)
    qkv_grad = weight_grad(over(normed1, 0), projected_all, 0, shard, ctx)

    def row_sum(items):
        return sum(jnp.sum(item.astype(jnp.float32), axis=0) for item in items)

    small = jnp.concatenate(
        [
            jnp.sum(projected_all[:width].astype(jnp.float32), axis=1),
            jnp.sum(projected_all[2 * width :].astype(jnp.float32), axis=1),
            row_sum(hidden_grads),
            row_sum(mixed_grads),
            row_sum([normed2_grads[m] * hats2[m][0] for m in range(micros)]),
            row_sum(normed2_grads),
            row_sum([cotangent[m, 0] for m in range(micros)]),
        ]
    )
    first = jnp.concatenate([sum(gain1), sum(bias1)])
    first = pair_sum(first, "tp", tp)
    small = jnp.concatenate([small, first])
    small = pair_sum(pair_sum(small, "ctx", ctx), "shard", shard)
    model = norm1_gain.shape[0]
    cuts, at = [], 0
    for count in (width, width, up_bias.shape[0], model, model, model, model, model, model):
        cuts.append(small[at : at + count])
        at += count
    query_bias_sum, value_bias_sum, up_bias_sum, out_bias_sum, gain2_sum, bias2_sum, down_bias_sum, gain1_sum, bias1_sum = cuts
    return (
        jnp.stack(outputs)[:, None],
        jnp.stack(input_grads)[:, None],
        gain1_sum,
        bias1_sum,
        qkv_grad[:, :width],
        query_bias_sum,
        qkv_grad[:, width : 2 * width],
        qkv_grad[:, 2 * width :],
        value_bias_sum,
        out_grad,
        out_bias_sum,
        gain2_sum,
        bias2_sum,
        up_grad,
        up_bias_sum,
        down_grad,
        down_bias_sum,
    )


def solution(mesh):
    sizes = (mesh.shape["shard"], mesh.shape["ctx"], mesh.shape["tp"])
    rows, weight, hidden, copied = P(None, "shard", "ctx", None), P("shard", "tp"), P("tp"), P()
    return jax.shard_map(
        functools.partial(body, sizes),
        mesh=mesh,
        in_specs=(
            rows,
            P(None, "shard"),
            copied,
            copied,
            weight,
            hidden,
            weight,
            weight,
            hidden,
            weight,
            copied,
            copied,
            copied,
            weight,
            hidden,
            weight,
            copied,
            rows,
        ),
        out_specs=(
            rows,
            rows,
            copied,
            copied,
            weight,
            hidden,
            weight,
            weight,
            hidden,
            weight,
            copied,
            copied,
            copied,
            weight,
            hidden,
            weight,
            copied,
        ),
        check_vma=False,
    )
```

```python
import functools
import math

import jax
import jax.numpy as jnp
from jax import lax
from jax.experimental import pallas as pl
from jax.experimental.pallas import tpu as pltpu
from jax.sharding import PartitionSpec as P

HEAD_DIM = 80
STEP = 512
SUB = 256
EPSILON = 1e-05
SCALE = HEAD_DIM**-0.5
LOW = jnp.bfloat16


def contract(left, right, dims):
    return lax.dot_general(left, right, (dims, ((), ())), preferred_element_type=jnp.float32)

class Weight:
    def __init__(self, index, piece, full, shard, split, ctx_index):
        self.index, self.piece, self.full, self.split = index, piece, full, split
        self.each = full.shape[-2] // shard
        self.rows = self.each // split
        self.part = lax.rem(ctx_index, split)

    def slice(self, shard_index, part):
        rows = pl.ds(pl.multiple_of(shard_index * self.each + part * self.rows, 16), self.rows)
        return self.full.at[:, rows] if len(self.full.shape) == 3 else self.full.at[rows]


def flip(index, bit):
    return index + bit - 2 * bit * lax.rem(index // bit, 2)


def opening_kernel(
    sizes,
    valid_ref,
    normed_ref,
    bias_ref,
    qkv_ref,
    out_ref,
    up_ref,
    down_ref,
    full_qkv,
    full_out,
    full_up,
    full_down,
    q_ref,
    kv_ref,
    a_ref,
    e_ref,
    inverse_ref,
    weights_ref,
    pairs_ref,
    mine_ref,
    s_ref,
    low_ref,
    z_send,
    z_recv,
    x_send,
    x_recv,
    c_send,
    c_recv,
    y_send,
    y_recv,
    kv_send,
    kv_recv,
    a_send,
    a_recv,
    own_sem,
    e_sem,
    last_sem,
):
    shard, ctx, tp = sizes
    width, rows = q_ref.shape[1], q_ref.shape[2]
    heads = width // HEAD_DIM
    i, p, me = lax.axis_index("shard"), lax.axis_index("ctx"), lax.axis_index("tp")
    across, beside = flip(p, 2), flip(p, 1)

    def remote(source, target, send, recv, **device):
        return pltpu.make_async_remote_copy(
            src_ref=source, dst_ref=target, send_sem=send, recv_sem=recv,
            device_id=device, device_id_type=pl.DeviceIdType.MESH,
        )

    def others():
        return [lax.rem(me + d, tp) for d in range(1, tp)]

    barrier = pltpu.get_barrier_semaphore()

    def greet(**device):
        pl.semaphore_signal(barrier, inc=1, device_id=device, device_id_type=pl.DeviceIdType.MESH)

    pl.when(i > 0)(lambda: greet(shard=i - 1))
    pl.when(i < shard - 1)(lambda: greet(shard=i + 1))
    greet(ctx=across)
    greet(ctx=beside)
    for other in others():
        greet(tp=other)
    pl.semaphore_wait(barrier, 2 + (tp - 1) + jnp.where(i > 0, 1, 0) + jnp.where(i < shard - 1, 1, 0))

    qkv = Weight(0, qkv_ref, weights_ref, shard, 4, p)
    out = Weight(1, out_ref, full_out, shard, 4, p)
    up = Weight(2, up_ref, full_up, shard, 4, p)
    down = Weight(3, down_ref, full_down, shard, 2, p)
    everything = (qkv, out, up, down)

    def z_copy(w, j, way):
        there = w.slice(j, w.part)
        return remote(there, there, z_send.at[w.index, (way + 1) // 2, j], z_recv.at[w.index, j], shard=i + way)

    def x_copy(w, j):
        there = w.slice(j, w.part)
        return remote(there, there, x_send.at[w.index, j], x_recv.at[w.index, j], ctx=across)

    def c_copy(w, j, which):
        there = w.slice(j, flip(w.part, 2) if which else w.part)
        return remote(there, there, c_send.at[w.index, j, which], c_recv.at[w.index, j, which], ctx=beside)

    def x_arriving(w, j):
        there = w.slice(j, flip(w.part, 2))
        return remote(there, there, x_send.at[w.index, j], x_recv.at[w.index, j], ctx=across)

    def c_arriving(w, j, which):
        there = w.slice(j, flip(flip(w.part, 2) if which else w.part, 1))
        return remote(there, there, c_send.at[w.index, j, which], c_recv.at[w.index, j, which], ctx=beside)

    def share(w, j):
        if w.split == 4:
            x_copy(w, j).start()
        c_copy(w, j, 0).start()

    def begin(w):
        pl.when(i < shard - 1)(lambda: z_copy(w, i, 1).start())
        pl.when(i > 0)(lambda: z_copy(w, i, -1).start())
        share(w, i)

    def arrive(w, hop):
        for way, there, j in ((1, i >= hop, i - hop), (-1, i + hop < shard, i + hop)):

            @pl.when(there)
            def _():
                z_copy(w, j, way).wait_recv()
                onward = (i < shard - 1) if way == 1 else (i > 0)
                pl.when(onward)(lambda: z_copy(w, j, way).start())
                share(w, j)

    def cross(w):
        def one(j, carry):
            x_arriving(w, j).wait_recv()
            c_copy(w, j, 1).start()
            return carry

        if w.split == 4:
            lax.fori_loop(0, shard, one, 0)

    def settle(w):
        def one(j, carry):
            c_arriving(w, j, 0).wait_recv()
            if w.split == 4:
                c_arriving(w, j, 1).wait_recv()
            return carry

        lax.fori_loop(0, shard, one, 0)

    def drain(w):
        def one(j, carry):
            pl.when((j <= i) & (i < shard - 1))(lambda: z_copy(w, j, 1).wait_send())
            pl.when((j >= i) & (i > 0))(lambda: z_copy(w, j, -1).wait_send())
            c_copy(w, j, 0).wait_send()
            if w.split == 4:
                x_copy(w, j).wait_send()
                c_copy(w, j, 1).wait_send()
            return carry

        lax.fori_loop(0, shard, one, 0)

    def own_copy(w):
        source = w.piece.at[pl.ds(pl.multiple_of(w.part * w.rows, 16), w.rows)]
        target = w.slice(i, w.part)
        if w is out:
            target = target.at[me]
        return pltpu.make_async_copy(source, target, own_sem.at[w.index])

    for w in everything:
        own_copy(w).start()
    own_copy(qkv).wait()
    begin(qkv)

    def y_copy(source_me, other, slot):
        there = out.slice(i, out.part).at[source_me]
        return remote(there, there, y_send.at[slot], y_recv.at[slot], tp=other)

    own_copy(out).wait()
    for d in range(1, tp):
        y_copy(me, lax.rem(me + d, tp), d).start()
    own_copy(up).wait()
    own_copy(down).wait()
    for hop in range(1, shard):
        if hop == shard - 1:
            for d in range(1, tp):
                y_copy(lax.rem(me + tp - d, tp), lax.rem(me + tp - d, tp), d).wait_recv()
            begin(out)
            begin(up)
        arrive(qkv, hop)
    cross(qkv)
    settle(qkv)
    keep_qkv = pltpu.make_async_copy(weights_ref, full_qkv, last_sem.at[0])
    keep_qkv.start()

    def project(m):
        columns = slice(m * rows, (m + 1) * rows)
        for which in range(3):
            for low in range(0, width, 256):
                high = min(width, low + 256)
                picked = slice(which * width + low, which * width + high)
                value = contract(weights_ref[:, picked], normed_ref[:, columns], ((0,), (0,))) + bias_ref[picked, 0:1]
                if which == 0:
                    q_ref[m, low:high] = (value * (SCALE * math.log2(math.e))).astype(LOW)
                else:
                    pairs_ref[m, 0, (which - 1) * width + low : (which - 1) * width + high] = value.astype(LOW)

    def kv_copy(m, source, target, to):
        return remote(
            pairs_ref.at[m, source], pairs_ref.at[m, target], kv_send.at[m, target - 1], kv_recv.at[m, target - 1], ctx=to
        )

    def send_pair(m):
        kv_copy(m, 0, 2, across).start()
        kv_copy(m, 0, 1, beside).start()

    def take_pair(m):
        kv_copy(m, 0, 2, across).wait_recv()
        kv_copy(m, 2, 3, beside).start()
        kv_copy(m, 0, 1, beside).wait_recv()
        kv_copy(m, 2, 3, beside).wait_recv()

    def e_copy(m, h):
        slot = lax.rem(h, 2)
        return pltpu.make_async_copy(low_ref.at[slot], e_ref.at[m, h], e_sem.at[slot])

    def attend(m, first, last):
        def one(h, carry):
            lanes = pl.ds(pl.multiple_of(h * HEAD_DIM, 16), HEAD_DIM)
            values = pl.ds(pl.multiple_of(width + h * HEAD_DIM, 16), HEAD_DIM)
            slot = lax.rem(h, 2)
            if m > 0:
                e_copy(m, h).wait()
            else:
                pl.when(h >= 2)(lambda: e_copy(m, h).wait())
            q = q_ref[m, lanes]
            top = jnp.full((1, rows), -1e30, jnp.float32)
            for b in range(ctx):
                s = contract(pairs_ref[m, b, lanes], q, ((0,), (0,)))
                at = lax.broadcasted_iota(jnp.int32, (rows, 1), 0)
                s = jnp.where(at < valid_ref[m, b], s, -1e30)
                s_ref[b] = s
                top = jnp.maximum(top, jnp.max(s, axis=0, keepdims=True))
            norm = jnp.zeros((1, rows), jnp.float32)
            total = jnp.zeros((HEAD_DIM, rows), jnp.float32)
            for b in range(ctx):
                e = jnp.exp2(s_ref[b] - top)
                norm = norm + jnp.sum(e, axis=0, keepdims=True)
                low = e.astype(LOW)
                low_ref[slot, b * rows : (b + 1) * rows] = low
                total = total + contract(pairs_ref[m, b, values], low, ((1,), (0,)))
            inverse = 1.0 / norm
            mine_ref[m, lanes] = (total * inverse).astype(LOW)
            inverse_ref[m, h] = jnp.broadcast_to(inverse, (8, rows))
            e_copy(m, h).start()
            return carry

        lax.fori_loop(first, last, one, 0)

    def a_copy(m, slot, other):
        return remote(mine_ref.at[m], a_ref.at[m, me], a_send.at[m, slot], a_recv.at[m, slot], tp=other)

    def a_arriving(m, slot, other):
        return remote(mine_ref.at[m], a_ref.at[m, other], a_send.at[m, slot], a_recv.at[m, slot], tp=other)

    def send_attended(m):
        for d in range(1, tp):
            a_copy(m, d, lax.rem(me + d, tp)).start()
        pltpu.make_async_copy(mine_ref.at[m], a_ref.at[m, me], last_sem.at[1 + m]).start()

    half = heads // 2
    project(0)
    send_pair(0)
    project(1)
    for hop in range(1, shard):
        arrive(out, hop)
    begin(down)
    arrive(up, 1)
    cross(out)
    take_pair(0)
    send_pair(1)
    arrive(up, 2)
    attend(0, 0, half)
    arrive(up, 3)
    attend(0, half, heads)
    send_attended(0)
    keep_pairs = [pltpu.make_async_copy(pairs_ref.at[m], kv_ref.at[m], last_sem.at[3 + m]) for m in range(2)]
    keep_pairs[0].start()
    arrive(down, 1)
    cross(up)
    take_pair(1)
    attend(1, 0, half)
    arrive(down, 2)
    attend(1, half, heads)
    send_attended(1)
    keep_pairs[1].start()
    arrive(down, 3)
    settle(out)
    settle(up)
    settle(down)
    for w in everything:
        drain(w)
    for d in range(1, tp):
        y_copy(me, lax.rem(me + d, tp), d).wait_send()
    for m in range(2):
        kv_copy(m, 0, 2, across).wait_send()
        kv_copy(m, 0, 1, beside).wait_send()
        kv_copy(m, 2, 3, beside).wait_send()
        for d in range(1, tp):
            a_arriving(m, d, lax.rem(me + tp - d, tp)).wait_recv()
            a_copy(m, d, lax.rem(me + d, tp)).wait_send()
        pltpu.make_async_copy(mine_ref.at[m], a_ref.at[m, me], last_sem.at[1 + m]).wait()
        keep_pairs[m].wait()
    keep_qkv.wait()
    for h in (heads - 2, heads - 1):
        e_copy(1, h).wait()


def opening(sizes, valid, normed, bias, qkv, out, up, down):
    shard, ctx, tp = sizes
    width = qkv.shape[1] // 3
    model = qkv.shape[0] * shard
    rows = normed.shape[1] // 2
    heads = width // HEAD_DIM
    low = lambda *shape: jax.ShapeDtypeStruct(shape, LOW)
    anywhere, vmem = pl.BlockSpec(memory_space=pl.ANY), pl.BlockSpec(memory_space=pltpu.VMEM)
    dma = pltpu.SemaphoreType.DMA
    keys = ctx * rows
    return pl.pallas_call(
        functools.partial(opening_kernel, sizes),
        in_specs=[pl.BlockSpec(memory_space=pltpu.SMEM), vmem, vmem] + [anywhere] * 4,
        out_specs=[anywhere] * 4 + [vmem, anywhere, anywhere, anywhere, vmem],
        out_shape=[
            low(model, 3 * width),
            low(tp, model, width),
            low(model, up.shape[1]),
            low(model, down.shape[1]),
            low(2, width, rows),
            low(2, ctx, 2 * width, rows),
            low(2, tp, width, rows),
            low(2, heads, keys, rows),
            jax.ShapeDtypeStruct((2, heads, 8, rows), jnp.float32),
        ],
        scratch_shapes=[
            pltpu.VMEM((model, 3 * width), LOW),
            pltpu.VMEM((2, ctx, 2 * width, rows), LOW),
            pltpu.VMEM((2, width, rows), LOW),
            pltpu.VMEM((ctx, rows, rows), jnp.float32),
            pltpu.VMEM((2, keys, rows), LOW),
            dma((4, 2, shard)),
            dma((4, shard)),
            dma((4, shard)),
            dma((4, shard)),
            dma((4, shard, 2)),
            dma((4, shard, 2)),
            dma((tp,)),
            dma((tp,)),
            dma((2, 3)),
            dma((2, 3)),
            dma((2, tp)),
            dma((2, tp)),
            dma((4,)),
            dma((2,)),
            dma((5,)),
        ],
        compiler_params=pltpu.CompilerParams(collective_id=0, has_side_effects=True, vmem_limit_bytes=56 << 20),
        cost_estimate=pl.CostEstimate(
            flops=8 * heads * rows * keys * 256, bytes_accessed=80 << 20, transcendentals=2 * heads * rows * keys
        ),
        name="opening",
    )(valid, normed, bias, qkv, out, up, down)


def backward_kernel(valid_ref, q_ref, g_ref, a_ref, inverse_ref, e_ref, *refs, blocks):
    k_refs, v_refs = refs[:blocks], refs[blocks:2*blocks]
    dq_ref = refs[2*blocks]
    dk_refs, dv_refs = refs[2*blocks+1:3*blocks+1], refs[3*blocks+1:4*blocks+1]
    acc_ref = refs[4*blocks+1]
    q = q_ref[...]
    g32 = g_ref[...].astype(jnp.float32) * inverse_ref[0, 0:1]
    delta = jnp.sum(g32 * a_ref[...].astype(jnp.float32), axis=0, keepdims=True)
    g = g32.astype(jnp.bfloat16)
    span = k_refs[0].shape[1]
    step=min(STEP,span)
    acc_ref[...] = jnp.zeros(acc_ref.shape, jnp.float32)
    for b in range(blocks):
        for off in range(0, span, step):
            left = valid_ref[b] - off
            cols = slice(off, off+step)
            rows = slice(b*span+off, b*span+off+step)
            def work():
                sub = min(SUB, step)
                parts = [(slice(off+o, off+o+sub), slice(b*span+off+o, b*span+off+o+sub)) for o in range(0, step, sub)]
                dps = [contract(v_refs[b][:, c], g, ((0,), (0,))) for c, r in parts]
                total = None
                for (c, r), dp in zip(parts, dps):
                    e = e_ref[0, r]
                    dv_refs[b][:, c] = contract(g, e, ((1,), (1,))).astype(jnp.bfloat16)
                    ds = (e.astype(jnp.float32) * (dp - delta)).astype(jnp.bfloat16)
                    t = contract(k_refs[b][:, c], ds, ((1,), (0,)))
                    total = t if total is None else total + t
                    dk_refs[b][:, c] = (contract(q, ds, ((1,), (1,))) * math.log(2.0)).astype(jnp.bfloat16)
                acc_ref[...] += total
            work()
    dq_ref[...] = (acc_ref[...] * HEAD_DIM**-0.5).astype(jnp.bfloat16)

def attention_backward(valid, q, g, a, inverse, e, kv):
    width, rows = q.shape
    heads = width // HEAD_DIM
    blocks, span = len(kv), kv[0].shape[1]
    head = lambda h: (h, 0)
    value = lambda h: (heads + h, 0)
    hspec = pl.BlockSpec((HEAD_DIM, rows), head)
    kspec = pl.BlockSpec((HEAD_DIM, span), head)
    vspec = pl.BlockSpec((HEAD_DIM, span), value)
    out = jax.ShapeDtypeStruct((width, span), jnp.bfloat16)
    return pl.pallas_call(
        functools.partial(backward_kernel, blocks=blocks),
        grid=(heads,),
        in_specs=[pl.BlockSpec(memory_space=pltpu.SMEM), hspec, hspec, hspec, pl.BlockSpec((1,8,rows), lambda h:(h,0,0)), pl.BlockSpec((1, blocks*span, rows), lambda h:(h,0,0))]
          + [kspec]*blocks + [vspec]*blocks,
        out_specs=[hspec] + [kspec]*(2*blocks),
        out_shape=[jax.ShapeDtypeStruct((width, rows), jnp.bfloat16)] + [out]*(2*blocks),
        scratch_shapes=[pltpu.VMEM((HEAD_DIM, rows), jnp.float32)],
        compiler_params=pltpu.CompilerParams(vmem_limit_bytes=40<<20),
        cost_estimate=pl.CostEstimate(flops=8*rows*blocks*span*256*heads, bytes_accessed=heads*blocks*span*rows*2, transcendentals=0),
        name="attention_backward",
    )(valid, q, g, a, inverse, e, *kv, *kv)


def swap(value, axis, bit, size):
    return lax.ppermute(value, axis, [(k, k ^ bit) for k in range(size)])


def bits_of(size):
    found, bit = [], size // 2
    while bit > 0:
        found.append(bit)
        bit //= 2
    return found


def spread(value, axis, size):
    blocks = {0: value}
    for bit in bits_of(size):
        blocks.update({mask | bit: swap(blocks[mask], axis, bit, size) for mask in list(blocks)})
    return [blocks[mask] for mask in range(size)]


def pair_sum(value, axis, size):
    for bit in reversed(bits_of(size)):
        value = value + swap(value, axis, bit, size)
    return value


def low_sum(value, axis, size):
    if size == 1:
        return value
    total = value.astype(LOW)
    for bit in reversed(bits_of(size)):
        total = (total.astype(jnp.float32) + swap(total, axis, bit, size).astype(jnp.float32)).astype(LOW)
    return total.astype(jnp.float32)


def canonical(blocks, axis, size):
    me = lax.axis_index(axis)
    out = jnp.zeros((size,) + blocks[0].shape, blocks[0].dtype)
    for mask, block in enumerate(blocks):
        out = lax.dynamic_update_index_in_dim(out, block, me ^ mask, 0)
    return out


def scatter_ctx(chunk, ctx):
    def total(mask, bits):
        if len(bits) == 0:
            return chunk(mask)
        bit, rest = bits[0], bits[1:]
        away = total(mask | bit, rest).astype(LOW)
        return total(mask, rest) + swap(away, "ctx", bit, ctx).astype(jnp.float32)

    return total(0, bits_of(ctx))


def scatter_rows(full, size):
    me = lax.axis_index("shard")
    rows = full.shape[0] // size
    total = lax.dynamic_slice_in_dim(full, me * rows, rows, 0)
    low = full.astype(LOW)
    for shift in range(1, size):
        there = lax.rem(me + shift, size)
        block = lax.dynamic_slice_in_dim(low, there * rows, rows, 0)
        got = lax.ppermute(block, "shard", [(k, (k + shift) % size) for k in range(size)])
        total = total + got.astype(jnp.float32)
    return total


def weight_grad(left, right, right_dim, shard, ctx):
    count = right.shape[right_dim] // ctx
    me = lax.axis_index("ctx")

    def chunk(mask):
        part = lax.dynamic_slice_in_dim(right, (me ^ mask) * count, count, right_dim)
        return contract(left, part, ((0,), (1 - right_dim,)))

    mine = scatter_rows(scatter_ctx(chunk, ctx), shard).astype(LOW)
    blocks = canonical(spread(mine, "ctx", ctx), "ctx", ctx)
    return jnp.moveaxis(blocks, 0, 1).reshape(mine.shape[0], ctx * count).astype(jnp.float32)


def normalize(values):
    center = values - jnp.mean(values, axis=-1, keepdims=True)
    spread_of = jnp.mean(center * center, axis=-1, keepdims=True)
    inverse = lax.rsqrt(spread_of + EPSILON)
    return center * inverse, inverse


def normalize_grad(grad, hat, inverse):
    return inverse * (
        grad - jnp.mean(grad, axis=-1, keepdims=True) - hat * jnp.mean(grad * hat, axis=-1, keepdims=True)
    )


def body(
    sizes,
    frames,
    lengths,
    norm1_gain,
    norm1_bias,
    query_weight,
    query_bias,
    key_weight,
    value_weight,
    value_bias,
    out_weight,
    out_bias,
    norm2_gain,
    norm2_bias,
    up_weight,
    up_bias,
    down_weight,
    down_bias,
    cotangent,
):
    shard, ctx, tp = sizes
    micros, rows = frames.shape[0], frames.shape[2]
    width = query_weight.shape[1]
    ctx_index = lax.axis_index("ctx")

    inputs = [frames[m, 0].astype(jnp.float32) for m in range(micros)]
    hats1 = [normalize(x) for x in inputs]
    normed1 = [(hat * norm1_gain + norm1_bias).astype(LOW) for hat, _ in hats1]
    bias = jnp.concatenate([query_bias, jnp.zeros_like(query_bias), value_bias])[:, None]
    ids = ctx_index ^ jnp.arange(ctx, dtype=jnp.int32)
    valid = [jnp.clip(lengths[m, 0] - rows * ids, 0, rows) for m in range(micros)]
    full_qkv, full_out, full_up, full_down, queries, pairs, all_attended, kept, inverses = opening(
        sizes,
        jnp.stack(valid),
        jnp.concatenate(normed1, axis=0).T,
        bias,
        jnp.concatenate([query_weight, key_weight, value_weight], axis=1),
        out_weight,
        up_weight,
        down_weight,
    )
    tp_index = lax.axis_index("tp")
    own_out = lax.dynamic_index_in_dim(full_out, tp_index, 0, keepdims=False)
    attended = [lax.dynamic_index_in_dim(all_attended[m], tp_index, 0, keepdims=False) for m in range(micros)]
    mixed, hats2, normed2, hidden = [], [], [], []
    for m in range(micros):
        branch = sum(contract(all_attended[m, t], full_out[t], ((0,), (1,))) for t in range(tp))
        mixed.append(inputs[m] + branch + out_bias)
        hats2.append(normalize(mixed[m]))
        normed2.append((hats2[m][0] * norm2_gain + norm2_bias).astype(LOW))
        hidden.append(contract(normed2[m], full_up, ((1,), (0,))) + up_bias)
    active, hidden_grads, outputs, mixed_grads, branch_grads = [], [], [], [], []
    normed2_grads = []
    for m in range(micros):
        cdf = 0.5 * (1.0 + lax.erf(hidden[m] * math.sqrt(0.5)))
        pdf = jnp.exp(-0.5 * hidden[m] * hidden[m]) * (1.0 / math.sqrt(2.0 * math.pi))
        active.append((hidden[m] * cdf).astype(LOW))
        slope = cdf + hidden[m] * pdf
        hidden_grads.append((contract(cotangent[m, 0], full_down, ((1,), (0,))) * slope).astype(LOW))
        normed2_grads.append(low_sum(contract(hidden_grads[m], full_up, ((1,), (1,))), "tp", tp))
    for m in range(micros):
        branch = low_sum(contract(active[m], full_down, ((1,), (1,))), "tp", tp)
        outputs.append((mixed[m] + branch + down_bias).astype(LOW))
        hat, inverse = hats2[m]
        mixed_grads.append(
            cotangent[m, 0].astype(jnp.float32) + normalize_grad(normed2_grads[m] * norm2_gain, hat, inverse)
        )
        branch_grads.append(mixed_grads[m].astype(LOW))
    projected_grads, normed1_terms, input_grads = [], [], []
    for m in range(micros):
        attended_grad = contract(own_out, branch_grads[m], ((0,), (1,))).astype(LOW)
        parts = attention_backward(
            valid[m], queries[m], attended_grad, attended[m], inverses[m], kept[m], [pairs[m, b] for b in range(ctx)]
        )
        terms = [
            jnp.concatenate([parts[1 + mask], parts[1 + ctx + mask]], axis=0) for mask in range(ctx)
        ]
        pair_grad = scatter_ctx(lambda mask: terms[mask].astype(jnp.float32), ctx).astype(LOW)
        projected_grads.append(jnp.concatenate([parts[0], pair_grad], axis=0))
        normed1_terms.append(contract(projected_grads[m], full_qkv, ((0,), (1,))))
    gain1, bias1 = [], []
    for m in range(micros):
        hat, inverse = hats1[m]
        gain1.append(jnp.sum(normed1_terms[m] * hat, axis=0))
        bias1.append(jnp.sum(normed1_terms[m], axis=0))
        total = low_sum(normed1_terms[m], "tp", tp)
        input_grads.append(mixed_grads[m] + normalize_grad(total * norm1_gain, hat, inverse))

    def over(items, dim):
        return jnp.concatenate(items, axis=dim)

    up_grad = weight_grad(over(normed2, 0), over(hidden_grads, 0), 1, shard, ctx)
    down_grad = weight_grad(over([cotangent[m, 0] for m in range(micros)], 0), over(active, 0), 1, shard, ctx)
    out_grad = weight_grad(over(branch_grads, 0), over(attended, 1), 0, shard, ctx)
    projected_all = over(projected_grads, 1)
    qkv_grad = weight_grad(over(normed1, 0), projected_all, 0, shard, ctx)

    def row_sum(items):
        return sum(jnp.sum(item.astype(jnp.float32), axis=0) for item in items)

    small = jnp.concatenate(
        [
            jnp.sum(projected_all[:width].astype(jnp.float32), axis=1),
            jnp.sum(projected_all[2 * width :].astype(jnp.float32), axis=1),
            row_sum(hidden_grads),
            row_sum(mixed_grads),
            row_sum([normed2_grads[m] * hats2[m][0] for m in range(micros)]),
            row_sum(normed2_grads),
            row_sum([cotangent[m, 0] for m in range(micros)]),
        ]
    )
    first = jnp.concatenate([sum(gain1), sum(bias1)])
    first = pair_sum(first, "tp", tp)
    small = jnp.concatenate([small, first])
    small = pair_sum(pair_sum(small, "ctx", ctx), "shard", shard)
    model = norm1_gain.shape[0]
    cuts, at = [], 0
    for count in (width, width, up_bias.shape[0], model, model, model, model, model, model):
        cuts.append(small[at : at + count])
        at += count
    query_bias_sum, value_bias_sum, up_bias_sum, out_bias_sum, gain2_sum, bias2_sum, down_bias_sum, gain1_sum, bias1_sum = cuts
    return (
        jnp.stack(outputs)[:, None],
        jnp.stack(input_grads)[:, None],
        gain1_sum,
        bias1_sum,
        qkv_grad[:, :width],
        query_bias_sum,
        qkv_grad[:, width : 2 * width],
        qkv_grad[:, 2 * width :],
        value_bias_sum,
        out_grad,
        out_bias_sum,
        gain2_sum,
        bias2_sum,
        up_grad,
        up_bias_sum,
        down_grad,
        down_bias_sum,
    )


def solution(mesh):
    sizes = (mesh.shape["shard"], mesh.shape["ctx"], mesh.shape["tp"])
    rows, weight, hidden, copied = P(None, "shard", "ctx", None), P("shard", "tp"), P("tp"), P()
    return jax.shard_map(
        functools.partial(body, sizes),
        mesh=mesh,
        in_specs=(
            rows,
            P(None, "shard"),
            copied,
            copied,
            weight,
            hidden,
            weight,
            weight,
            hidden,
            weight,
            copied,
            copied,
            copied,
            weight,
            hidden,
            weight,
            copied,
            rows,
        ),
        out_specs=(
            rows,
            rows,
            copied,
            copied,
            weight,
            hidden,
            weight,
            weight,
            hidden,
            weight,
            copied,
            copied,
            copied,
            weight,
            hidden,
            weight,
            copied,
        ),
        check_vma=False,
    )
```

```python
import functools
import math

import jax
import jax.numpy as jnp
from jax import lax
from jax.experimental import pallas as pl
from jax.experimental.pallas import tpu as pltpu
from jax.sharding import PartitionSpec as P

HEAD_DIM = 80
STEP = 512
SUB = 256
EPSILON = 1e-05
SCALE = HEAD_DIM**-0.5
LOW = jnp.bfloat16


def contract(left, right, dims):
    return lax.dot_general(left, right, (dims, ((), ())), preferred_element_type=jnp.float32)

class Weight:
    def __init__(self, index, piece, full, shard, split, ctx_index):
        self.index, self.piece, self.full, self.split = index, piece, full, split
        self.each = full.shape[-2] // shard
        self.rows = self.each // split
        self.part = lax.rem(ctx_index, split)

    def slice(self, shard_index, part):
        rows = pl.ds(pl.multiple_of(shard_index * self.each + part * self.rows, 16), self.rows)
        return self.full.at[:, rows] if len(self.full.shape) == 3 else self.full.at[rows]


def flip(index, bit):
    return index + bit - 2 * bit * lax.rem(index // bit, 2)


def opening_kernel(
    sizes,
    valid_ref,
    normed_ref,
    bias_ref,
    qkv_ref,
    out_ref,
    up_ref,
    down_ref,
    full_qkv,
    full_out,
    full_up,
    full_down,
    q_ref,
    kv_ref,
    a_ref,
    e_ref,
    inverse_ref,
    weights_ref,
    pairs_ref,
    mine_ref,
    s_ref,
    low_ref,
    z_send,
    z_recv,
    x_send,
    x_recv,
    c_send,
    c_recv,
    y_send,
    y_recv,
    kv_send,
    kv_recv,
    a_send,
    a_recv,
    own_sem,
    e_sem,
    last_sem,
):
    shard, ctx, tp = sizes
    width, rows = q_ref.shape[1], q_ref.shape[2]
    heads = width // HEAD_DIM
    i, p, me = lax.axis_index("shard"), lax.axis_index("ctx"), lax.axis_index("tp")
    across, beside = flip(p, 2), flip(p, 1)

    def remote(source, target, send, recv, **device):
        return pltpu.make_async_remote_copy(
            src_ref=source, dst_ref=target, send_sem=send, recv_sem=recv,
            device_id=device, device_id_type=pl.DeviceIdType.MESH,
        )

    def others():
        return [lax.rem(me + d, tp) for d in range(1, tp)]

    barrier = pltpu.get_barrier_semaphore()

    def greet(**device):
        pl.semaphore_signal(barrier, inc=1, device_id=device, device_id_type=pl.DeviceIdType.MESH)

    pl.when(i > 0)(lambda: greet(shard=i - 1))
    pl.when(i < shard - 1)(lambda: greet(shard=i + 1))
    greet(ctx=across)
    greet(ctx=beside)
    for other in others():
        greet(tp=other)
    pl.semaphore_wait(barrier, 2 + (tp - 1) + jnp.where(i > 0, 1, 0) + jnp.where(i < shard - 1, 1, 0))

    qkv = Weight(0, qkv_ref, weights_ref, shard, 4, p)
    out = Weight(1, out_ref, full_out, shard, 4, p)
    up = Weight(2, up_ref, full_up, shard, 4, p)
    down = Weight(3, down_ref, full_down, shard, 2, p)
    everything = (qkv, out, up, down)

    def z_copy(w, j, way):
        there = w.slice(j, w.part)
        return remote(there, there, z_send.at[w.index, (way + 1) // 2, j], z_recv.at[w.index, j], shard=i + way)

    def x_copy(w, j):
        there = w.slice(j, w.part)
        return remote(there, there, x_send.at[w.index, j], x_recv.at[w.index, j], ctx=across)

    def c_copy(w, j, which):
        there = w.slice(j, flip(w.part, 2) if which else w.part)
        return remote(there, there, c_send.at[w.index, j, which], c_recv.at[w.index, j, which], ctx=beside)

    def x_arriving(w, j):
        there = w.slice(j, flip(w.part, 2))
        return remote(there, there, x_send.at[w.index, j], x_recv.at[w.index, j], ctx=across)

    def c_arriving(w, j, which):
        there = w.slice(j, flip(flip(w.part, 2) if which else w.part, 1))
        return remote(there, there, c_send.at[w.index, j, which], c_recv.at[w.index, j, which], ctx=beside)

    def share(w, j):
        if w.split == 4 and w is not up:
            x_copy(w, j).start()
        c_copy(w, j, 0).start()

    def push(w):
        def one(j, carry):
            x_copy(w, j).start()
            return carry

        lax.fori_loop(0, shard, one, 0)

    def begin(w):
        pl.when(i < shard - 1)(lambda: z_copy(w, i, 1).start())
        pl.when(i > 0)(lambda: z_copy(w, i, -1).start())
        share(w, i)

    def arrive(w, hop):
        for way, there, j in ((1, i >= hop, i - hop), (-1, i + hop < shard, i + hop)):

            @pl.when(there)
            def _():
                z_copy(w, j, way).wait_recv()
                onward = (i < shard - 1) if way == 1 else (i > 0)
                pl.when(onward)(lambda: z_copy(w, j, way).start())
                share(w, j)

    def cross(w):
        def one(j, carry):
            x_arriving(w, j).wait_recv()
            c_copy(w, j, 1).start()
            return carry

        if w.split == 4:
            lax.fori_loop(0, shard, one, 0)

    def settle(w):
        def one(j, carry):
            c_arriving(w, j, 0).wait_recv()
            if w.split == 4:
                c_arriving(w, j, 1).wait_recv()
            return carry

        lax.fori_loop(0, shard, one, 0)

    def drain(w):
        def one(j, carry):
            pl.when((j <= i) & (i < shard - 1))(lambda: z_copy(w, j, 1).wait_send())
            pl.when((j >= i) & (i > 0))(lambda: z_copy(w, j, -1).wait_send())
            c_copy(w, j, 0).wait_send()
            if w.split == 4:
                x_copy(w, j).wait_send()
                c_copy(w, j, 1).wait_send()
            return carry

        lax.fori_loop(0, shard, one, 0)

    def own_copy(w):
        target = w.slice(i, w.part)
        if w is out:
            target = target.at[me]
        return pltpu.make_async_copy(w.piece, target, own_sem.at[w.index])

    for w in everything:
        own_copy(w).start()
    own_copy(qkv).wait()
    begin(qkv)

    def y_copy(source_me, other, slot):
        there = out.slice(i, out.part).at[source_me]
        return remote(there, there, y_send.at[slot], y_recv.at[slot], tp=other)

    own_copy(out).wait()
    for d in range(1, tp):
        y_copy(me, lax.rem(me + d, tp), d).start()
    own_copy(up).wait()
    own_copy(down).wait()
    for hop in range(1, shard):
        if hop == shard - 1:
            for d in range(1, tp):
                y_copy(lax.rem(me + tp - d, tp), lax.rem(me + tp - d, tp), d).wait_recv()
            begin(out)
        arrive(qkv, hop)
    cross(qkv)
    settle(qkv)
    keep_qkv = pltpu.make_async_copy(weights_ref, full_qkv, last_sem.at[0])
    keep_qkv.start()

    def project(m):
        columns = slice(m * rows, (m + 1) * rows)
        for which in range(3):
            for low in range(0, width, 256):
                high = min(width, low + 256)
                picked = slice(which * width + low, which * width + high)
                value = contract(weights_ref[:, picked], normed_ref[:, columns], ((0,), (0,))) + bias_ref[picked, 0:1]
                if which == 0:
                    q_ref[m, low:high] = (value * (SCALE * math.log2(math.e))).astype(LOW)
                else:
                    pairs_ref[m, 0, (which - 1) * width + low : (which - 1) * width + high] = value.astype(LOW)

    def kv_copy(m, source, target, to):
        return remote(
            pairs_ref.at[m, source], pairs_ref.at[m, target], kv_send.at[m, target - 1], kv_recv.at[m, target - 1], ctx=to
        )

    def send_pair(m):
        kv_copy(m, 0, 2, across).start()
        kv_copy(m, 0, 1, beside).start()

    def take_pair(m):
        kv_copy(m, 0, 2, across).wait_recv()
        kv_copy(m, 2, 3, beside).start()
        kv_copy(m, 0, 1, beside).wait_recv()
        kv_copy(m, 2, 3, beside).wait_recv()

    def e_copy(m, h):
        slot = lax.rem(h, 2)
        return pltpu.make_async_copy(low_ref.at[slot], e_ref.at[m, h], e_sem.at[slot])

    def attend(m, first, last):
        def one(h, carry):
            lanes = pl.ds(pl.multiple_of(h * HEAD_DIM, 16), HEAD_DIM)
            values = pl.ds(pl.multiple_of(width + h * HEAD_DIM, 16), HEAD_DIM)
            slot = lax.rem(h, 2)
            if m > 0:
                e_copy(m, h).wait()
            else:
                pl.when(h >= 2)(lambda: e_copy(m, h).wait())
            q = q_ref[m, lanes]
            top = jnp.full((1, rows), -1e30, jnp.float32)
            for b in range(ctx):
                s = contract(pairs_ref[m, b, lanes], q, ((0,), (0,)))
                at = lax.broadcasted_iota(jnp.int32, (rows, 1), 0)
                s = jnp.where(at < valid_ref[m, b], s, -1e30)
                s_ref[b] = s
                top = jnp.maximum(top, jnp.max(s, axis=0, keepdims=True))
            norm = jnp.zeros((1, rows), jnp.float32)
            total = jnp.zeros((HEAD_DIM, rows), jnp.float32)
            for b in range(ctx):
                e = jnp.exp2(s_ref[b] - top)
                norm = norm + jnp.sum(e, axis=0, keepdims=True)
                low = e.astype(LOW)
                low_ref[slot, b * rows : (b + 1) * rows] = low
                total = total + contract(pairs_ref[m, b, values], low, ((1,), (0,)))
            inverse = 1.0 / norm
            mine_ref[m, lanes] = (total * inverse).astype(LOW)
            inverse_ref[m, h] = jnp.broadcast_to(inverse, (8, rows))
            e_copy(m, h).start()
            return carry

        lax.fori_loop(first, last, one, 0)

    def a_copy(m, slot, other):
        return remote(mine_ref.at[m], a_ref.at[m, me], a_send.at[m, slot], a_recv.at[m, slot], tp=other)

    def a_arriving(m, slot, other):
        return remote(mine_ref.at[m], a_ref.at[m, other], a_send.at[m, slot], a_recv.at[m, slot], tp=other)

    def send_attended(m):
        for d in range(1, tp):
            a_copy(m, d, lax.rem(me + d, tp)).start()
        pltpu.make_async_copy(mine_ref.at[m], a_ref.at[m, me], last_sem.at[1 + m]).start()

    half = heads // 2
    project(0)
    send_pair(0)
    project(1)
    for hop in range(1, shard):
        if hop == shard - 1:
            begin(up)
        arrive(out, hop)
    for hop in range(1, shard - 1):
        arrive(up, hop)
    begin(down)
    cross(out)
    take_pair(0)
    send_pair(1)
    arrive(up, shard - 1)
    push(up)
    attend(0, 0, half)
    arrive(down, 1)
    attend(0, half, heads)
    send_attended(0)
    keep_pairs = [pltpu.make_async_copy(pairs_ref.at[m], kv_ref.at[m], last_sem.at[3 + m]) for m in range(2)]
    keep_pairs[0].start()
    for hop in range(2, shard - 1):
        arrive(down, hop)
    take_pair(1)
    attend(1, 0, heads)
    send_attended(1)
    keep_pairs[1].start()
    cross(up)
    arrive(down, shard - 1)
    settle(out)
    settle(up)
    settle(down)
    for w in everything:
        drain(w)
    for d in range(1, tp):
        y_copy(me, lax.rem(me + d, tp), d).wait_send()
    for m in range(2):
        kv_copy(m, 0, 2, across).wait_send()
        kv_copy(m, 0, 1, beside).wait_send()
        kv_copy(m, 2, 3, beside).wait_send()
        for d in range(1, tp):
            a_arriving(m, d, lax.rem(me + tp - d, tp)).wait_recv()
            a_copy(m, d, lax.rem(me + d, tp)).wait_send()
        pltpu.make_async_copy(mine_ref.at[m], a_ref.at[m, me], last_sem.at[1 + m]).wait()
        keep_pairs[m].wait()
    keep_qkv.wait()
    for h in (heads - 2, heads - 1):
        e_copy(1, h).wait()


def opening(sizes, valid, normed, bias, qkv, out, up, down):
    shard, ctx, tp = sizes
    width = qkv.shape[1] // 3
    model = qkv.shape[0] * 4 * shard
    rows = normed.shape[1] // 2
    heads = width // HEAD_DIM
    low = lambda *shape: jax.ShapeDtypeStruct(shape, LOW)
    anywhere, vmem = pl.BlockSpec(memory_space=pl.ANY), pl.BlockSpec(memory_space=pltpu.VMEM)
    dma = pltpu.SemaphoreType.DMA
    keys = ctx * rows
    return pl.pallas_call(
        functools.partial(opening_kernel, sizes),
        in_specs=[pl.BlockSpec(memory_space=pltpu.SMEM)] + [vmem] * 6,
        out_specs=[anywhere] * 4 + [vmem, anywhere, anywhere, anywhere, vmem],
        out_shape=[
            low(model, 3 * width),
            low(tp, model, width),
            low(model, up.shape[1]),
            low(model, down.shape[1]),
            low(2, width, rows),
            low(2, ctx, 2 * width, rows),
            low(2, tp, width, rows),
            low(2, heads, keys, rows),
            jax.ShapeDtypeStruct((2, heads, 8, rows), jnp.float32),
        ],
        scratch_shapes=[
            pltpu.VMEM((model, 3 * width), LOW),
            pltpu.VMEM((2, ctx, 2 * width, rows), LOW),
            pltpu.VMEM((2, width, rows), LOW),
            pltpu.VMEM((ctx, rows, rows), jnp.float32),
            pltpu.VMEM((2, keys, rows), LOW),
            dma((4, 2, shard)),
            dma((4, shard)),
            dma((4, shard)),
            dma((4, shard)),
            dma((4, shard, 2)),
            dma((4, shard, 2)),
            dma((tp,)),
            dma((tp,)),
            dma((2, 3)),
            dma((2, 3)),
            dma((2, tp)),
            dma((2, tp)),
            dma((4,)),
            dma((2,)),
            dma((5,)),
        ],
        compiler_params=pltpu.CompilerParams(collective_id=0, has_side_effects=True, vmem_limit_bytes=56 << 20),
        cost_estimate=pl.CostEstimate(
            flops=8 * heads * rows * keys * 256, bytes_accessed=80 << 20, transcendentals=2 * heads * rows * keys
        ),
        name="opening",
    )(valid, normed, bias, qkv, out, up, down)


def backward_kernel(q_ref, g_ref, a_ref, inverse_ref, e_ref, pairs_ref, dq_ref, pairs_grad_ref, acc_ref):
    ctx, rows = pairs_ref.shape[1], pairs_ref.shape[4]
    q = q_ref[0]
    g32 = g_ref[...].astype(jnp.float32) * inverse_ref[0, 0, 0:1]
    delta = jnp.sum(g32 * a_ref[0, 0].astype(jnp.float32), axis=0, keepdims=True)
    g = g32.astype(LOW)
    sub = min(SUB, rows)
    acc_ref[...] = jnp.zeros(acc_ref.shape, jnp.float32)
    for b in range(ctx):
        to = (b % 2) * 2 + b // 2
        parts = [(slice(o, o + sub), slice(b * rows + o, b * rows + o + sub)) for o in range(0, rows, sub)]
        grads = [contract(pairs_ref[0, b, 1, :, c], g, ((0,), (0,))) for c, _ in parts]
        total = None
        for (c, r), grad in zip(parts, grads):
            e = e_ref[0, 0, r]
            pairs_grad_ref[to, 1, :, c] = contract(g, e, ((1,), (1,))).astype(LOW)
            ds = (e.astype(jnp.float32) * (grad - delta)).astype(LOW)
            term = contract(pairs_ref[0, b, 0, :, c], ds, ((1,), (0,)))
            total = term if total is None else total + term
            pairs_grad_ref[to, 0, :, c] = (contract(q, ds, ((1,), (1,))) * math.log(2.0)).astype(LOW)
        acc_ref[...] += total
    dq_ref[...] = (acc_ref[...] * SCALE).astype(LOW)


def attention_backward(micro, own, queries, grad, attended, inverses, kept, pairs):
    _, width, rows = queries.shape
    heads, ctx = width // HEAD_DIM, pairs.shape[1]
    keys = ctx * rows
    pairs = pairs.reshape(pairs.shape[0], ctx, 2, width, rows)
    grid = pltpu.PrefetchScalarGridSpec(
        num_scalar_prefetch=1,
        grid=(heads,),
        in_specs=[
            pl.BlockSpec((1, HEAD_DIM, rows), lambda h, own: (micro, h, 0)),
            pl.BlockSpec((HEAD_DIM, rows), lambda h, own: (h, 0)),
            pl.BlockSpec((1, 1, HEAD_DIM, rows), lambda h, own: (micro, own[0], h, 0)),
            pl.BlockSpec((1, 1, 8, rows), lambda h, own: (micro, h, 0, 0)),
            pl.BlockSpec((1, 1, keys, rows), lambda h, own: (micro, h, 0, 0)),
            pl.BlockSpec((1, ctx, 2, HEAD_DIM, rows), lambda h, own: (micro, 0, 0, h, 0)),
        ],
        out_specs=[
            pl.BlockSpec((HEAD_DIM, rows), lambda h, own: (h, 0)),
            pl.BlockSpec((ctx, 2, HEAD_DIM, rows), lambda h, own: (0, 0, h, 0)),
        ],
        scratch_shapes=[pltpu.VMEM((HEAD_DIM, rows), jnp.float32)],
    )
    return pl.pallas_call(
        lambda own_ref, *refs: backward_kernel(*refs),
        grid_spec=grid,
        out_shape=[
            jax.ShapeDtypeStruct((width, rows), LOW),
            jax.ShapeDtypeStruct((ctx, 2, width, rows), LOW),
        ],
        compiler_params=pltpu.CompilerParams(vmem_limit_bytes=40 << 20),
        cost_estimate=pl.CostEstimate(
            flops=8 * rows * keys * 256 * heads, bytes_accessed=heads * keys * rows * 2, transcendentals=0
        ),
        name="attention_backward",
    )(own, queries, grad, attended, inverses, kept, pairs)


def swap(value, axis, bit, size):
    return lax.ppermute(value, axis, [(k, k ^ bit) for k in range(size)])


def bits_of(size):
    found, bit = [], size // 2
    while bit > 0:
        found.append(bit)
        bit //= 2
    return found


def low_sum_start(value, axis, size):
    total = value.astype(LOW)
    if size == 1:
        return total, jnp.zeros_like(total)
    for bit in reversed(bits_of(size)):
        got = swap(total, axis, bit, size)
        if bit == size // 2:
            return total, got
        total = (total.astype(jnp.float32) + got.astype(jnp.float32)).astype(LOW)


def low_sum(value, axis, size):
    total, got = low_sum_start(value, axis, size)
    return (total.astype(jnp.float32) + got.astype(jnp.float32)).astype(LOW).astype(jnp.float32)


class Gradient:
    def __init__(self, index, across_first, terms, refs):
        self.index, self.across_first, self.terms = index, across_first, terms
        self.result, self.near, self.far, self.hops, self.crossed = refs
        self.sums = (self.near, self.far)
        self.halves = (0,) if across_first else (0, 1)


def closing_kernel(sizes, across_first, small_ref, first_ref, *refs):
    shard, ctx, tp = sizes
    units = len(across_first)
    terms, refs = refs[: 4 * units], refs[4 * units :]
    results, refs = refs[:units], refs[units:]
    small_out, first_out, refs = refs[0], refs[1], refs[2:]
    scratch, refs = refs[: 4 * units], refs[4 * units :]
    small_got, first_got, c_send, c_recv, x_send, x_recv, z_send, z_recv, g_send, g_recv, v_send, v_recv = refs
    i, p, me = lax.axis_index("shard"), lax.axis_index("ctx"), lax.axis_index("tp")
    across, beside = flip(p, 2), flip(p, 1)
    grads = [
        Gradient(u, across_first[u], terms[4 * u : 4 * u + 4], (results[u],) + tuple(scratch[4 * u : 4 * u + 4]))
        for u in range(units)
    ]

    def remote(source, target, send, recv, **device):
        return pltpu.make_async_remote_copy(
            src_ref=source, dst_ref=target, send_sem=send, recv_sem=recv,
            device_id=device, device_id_type=pl.DeviceIdType.MESH,
        )

    barrier = pltpu.get_barrier_semaphore()

    def greet(**device):
        pl.semaphore_signal(barrier, inc=1, device_id=device, device_id_type=pl.DeviceIdType.MESH)

    partners = [("tp", me, bit) for bit in reversed(bits_of(tp))]
    partners += [("ctx", p, bit) for bit in reversed(bits_of(ctx))]
    partners += [("shard", i, bit) for bit in reversed(bits_of(shard))]
    for axis, index, bit in partners:
        greet(**{axis: flip(index, bit)})
    skipped = jnp.where(i > 0, jnp.where(lax.rem(i, 2) == 0, 1, 0), 0)
    ahead = jnp.where(i < shard - 1, jnp.where(lax.rem(i, 2) == 1, 1, 0), 0)
    pl.when(skipped == 1)(lambda: greet(shard=i - 1))
    pl.when(ahead == 1)(lambda: greet(shard=i + 1))
    pl.semaphore_wait(barrier, len(partners) + skipped + ahead)

    def rows_of(ref, j):
        each = ref.shape[-2] // shard
        return ref.at[pl.ds(pl.multiple_of(j * each, 16), each)]

    def c_copy(g, j, which):
        source = g.terms[3 if which else 1]
        target = g.far if which else g.near
        return remote(
            rows_of(source, j), rows_of(target, j),
            c_send.at[g.index, j, which], c_recv.at[g.index, j, which], ctx=beside,
        )

    def x_copy(g, j):
        return remote(
            rows_of(g.sums[1], j), rows_of(g.crossed, j), x_send.at[g.index, j], x_recv.at[g.index, j], ctx=across
        )

    def z_copy(g, half, way, step, j):
        return remote(
            rows_of(g.sums[half], j), g.hops.at[half, way, step],
            z_send.at[g.index, half, way, step], z_recv.at[g.index, half, way, step], shard=i + 1 - 2 * way,
        )

    def add_to(target, value):
        target[...] = (target[...].astype(jnp.float32) + value.astype(jnp.float32)).astype(LOW)

    def every_shard(one):
        lax.fori_loop(0, shard, lambda j, carry: (one(j), carry)[1], 0)

    for g in grads:
        for j in range(shard):
            c_copy(g, j, 0).start()
            c_copy(g, j, 1).start()

    def meet(g, j):
        c_copy(g, j, 0).wait_recv()
        c_copy(g, j, 1).wait_recv()
        for half, got in ((0, g.near), (1, g.far)):
            add_to(rows_of(got, j), rows_of(g.terms[2 * half], j)[...])
        if g.across_first:
            x_copy(g, j).start()

    def joined(g, j):
        x_copy(g, j).wait_recv()
        add_to(rows_of(g.sums[0], j), rows_of(g.crossed, j)[...])

    def hop(g, step):
        for half in g.halves:
            for way, at in ((0, i), (1, shard - 1 - i)):
                j = shard - 1 - step + at if way == 0 else step - at

                @pl.when((at <= step) & (at < shard - 1))
                def _():
                    @pl.when(at > 0)
                    def _():
                        z_copy(g, half, way, step - 1, j).wait_recv()
                        add_to(rows_of(g.sums[half], j), g.hops[half, way, step - 1])

                    z_copy(g, half, way, step, j).start()

    def arrive(g):
        for half in g.halves:
            for way, at in ((0, i), (1, shard - 1 - i)):

                @pl.when(at > 0)
                def _():
                    z_copy(g, half, way, shard - 2, i).wait_recv()
                    add_to(rows_of(g.sums[half], i), g.hops[half, way, shard - 2])

    def side_copy(g):
        return remote(rows_of(g.sums[1], i), g.crossed, x_send.at[g.index, 0], x_recv.at[g.index, 0], ctx=across)

    def spread_copy(g, which):
        owner = across if which == 2 else p
        to = across if which == 0 else beside
        return remote(
            g.result.at[owner], g.result.at[owner], g_send.at[g.index, which], g_recv.at[g.index, which], ctx=to
        )

    def spread_arriving(g, which):
        owner = (across, beside, flip(across, 1))[which]
        to = across if which == 0 else beside
        return remote(
            g.result.at[owner], g.result.at[owner], g_send.at[g.index, which], g_recv.at[g.index, which], ctx=to
        )

    def finish(g):
        g.result[p] = rows_of(g.sums[0], i)[...]
        spread_copy(g, 0).start()
        spread_copy(g, 1).start()

    vectors = ((0, small_ref, small_out, small_got), (1, first_ref, first_out, first_got))

    def v_copy(number, which):
        axis, index, bit = partners[number]
        _, _, total, got = vectors[which]
        return remote(
            total.at[number], got.at[number], v_send.at[number, which], v_recv.at[number, which], **{axis: flip(index, bit)}
        )

    def meant(number):
        return (1,) if partners[number][0] == "tp" else (0, 1)

    def vector_start(number):
        for which in meant(number):
            v_copy(number, which).start()

    def vector_take(number):
        for which, _, total, got in vectors:
            if which in meant(number):
                v_copy(number, which).wait_recv()
                total[number + 1] = total[number] + got[number]
            else:
                total[number + 1] = total[number]

    small_out[0] = small_ref[...]
    first_out[0] = first_ref[...]
    vector_start(0)
    sent_across = [g for g in grads if g.across_first]
    sent_along = [g for g in grads if not g.across_first]
    for g in sent_across[:1] + sent_along + sent_across[1:]:
        every_shard(lambda j: meet(g, j))
        if not g.across_first:
            for step in range(1):
                hop(g, step)
    number = 0

    def next_vector():
        nonlocal number
        if number < len(partners):
            vector_take(number)
            number += 1
            if number < len(partners):
                vector_start(number)

    for step in range(1, shard - 1):
        for g in sent_along:
            hop(g, step)
        next_vector()
    for g in sent_across:
        every_shard(lambda j: joined(g, j))
        hop(g, 0)
        next_vector()
    for g in sent_along:
        arrive(g)
        side_copy(g).start()
    for step in range(1, shard - 1):
        for g in sent_across:
            hop(g, step)
        next_vector()
    for g in sent_along:
        side_copy(g).wait_recv()
        add_to(rows_of(g.sums[0], i), g.crossed[...])
        finish(g)
    for g in sent_across:
        arrive(g)
        finish(g)
    while number < len(partners):
        next_vector()
    for g in grads:
        spread_arriving(g, 0).wait_recv()
        spread_copy(g, 2).start()
    for g in grads:
        spread_arriving(g, 1).wait_recv()
        spread_arriving(g, 2).wait_recv()
    for g in grads:

        def drain(j):
            c_copy(g, j, 0).wait_send()
            c_copy(g, j, 1).wait_send()
            if g.across_first:
                x_copy(g, j).wait_send()

        every_shard(drain)
        if not g.across_first:
            side_copy(g).wait_send()
        for half in g.halves:
            for way, at in ((0, i), (1, shard - 1 - i)):
                for step in range(shard - 1):
                    j = shard - 1 - step + at if way == 0 else step - at

                    @pl.when((at <= step) & (at < shard - 1))
                    def _():
                        z_copy(g, half, way, step, j).wait_send()

        for which in range(3):
            spread_copy(g, which).wait_send()
    for n in range(len(partners)):
        for which in meant(n):
            v_copy(n, which).wait_send()


def closing(sizes, across_first, small, first, terms):
    shard, ctx, tp = sizes
    units = len(across_first)
    vmem = pl.BlockSpec(memory_space=pltpu.VMEM)
    dma = pltpu.SemaphoreType.DMA
    stages = len(bits_of(tp)) + len(bits_of(ctx)) + len(bits_of(shard))
    shapes = [t[0].shape for t in terms]
    scratch = []
    for (model, n), early in zip(shapes, across_first):
        each, halves = model // shard, 1 if early else 2
        scratch += [
            pltpu.VMEM((model, n), LOW),
            pltpu.VMEM((model, n), LOW),
            pltpu.VMEM((halves, 2, shard - 1, each, n), LOW),
            pltpu.VMEM((model, n) if early else (each, n), LOW),
        ]
    found = pl.pallas_call(
        functools.partial(closing_kernel, sizes, across_first),
        in_specs=[vmem] * (2 + 4 * units),
        out_specs=[vmem] * (units + 2),
        out_shape=[jax.ShapeDtypeStruct((ctx, model // shard, n), LOW) for model, n in shapes]
        + [jax.ShapeDtypeStruct((stages + 1,) + v.shape, jnp.float32) for v in (small, first)],
        scratch_shapes=scratch
        + [pltpu.VMEM((stages,) + v.shape, jnp.float32) for v in (small, first)]
        + [
            dma((units, shard, 2)),
            dma((units, shard, 2)),
            dma((units, shard)),
            dma((units, shard)),
            dma((units, 2, 2, shard - 1)),
            dma((units, 2, 2, shard - 1)),
            dma((units, 3)),
            dma((units, 3)),
            dma((stages, 2)),
            dma((stages, 2)),
        ],
        compiler_params=pltpu.CompilerParams(collective_id=1, has_side_effects=True, vmem_limit_bytes=56 << 20),
        cost_estimate=pl.CostEstimate(flops=0, bytes_accessed=200 << 20, transcendentals=0),
        name="closing",
    )(small, first, *[t for four in terms for t in four])
    return found[:units], found[units][stages], found[units + 1][stages]


def weight_terms(lefts, rights, right_dim, ctx):
    count = rights[0].shape[right_dim] // ctx
    me = lax.axis_index("ctx")

    def term(mask):
        total = 0.0
        for left, right in zip(lefts, rights):
            part = lax.dynamic_slice_in_dim(right, (me ^ mask) * count, count, right_dim)
            total = total + contract(left, part, ((0,), (1 - right_dim,)))
        return total.astype(LOW)

    return [term(mask) for mask in range(ctx)]


def whole_rows(blocks):
    ctx, each, n = blocks.shape
    return jnp.moveaxis(blocks, 0, 1).reshape(each, ctx * n).astype(jnp.float32)


def as_tiles(vector):
    count = -(-vector.shape[0] // 1024) * 1024
    return jnp.pad(vector, (0, count - vector.shape[0])).reshape(-1, 128)


def normalize(values):
    center = values - jnp.mean(values, axis=-1, keepdims=True)
    spread_of = jnp.mean(center * center, axis=-1, keepdims=True)
    inverse = lax.rsqrt(spread_of + EPSILON)
    return center * inverse, inverse


def normalize_grad(grad, hat, inverse):
    return inverse * (
        grad - jnp.mean(grad, axis=-1, keepdims=True) - hat * jnp.mean(grad * hat, axis=-1, keepdims=True)
    )


def body(
    sizes,
    frames,
    lengths,
    norm1_gain,
    norm1_bias,
    query_weight,
    query_bias,
    key_weight,
    value_weight,
    value_bias,
    out_weight,
    out_bias,
    norm2_gain,
    norm2_bias,
    up_weight,
    up_bias,
    down_weight,
    down_bias,
    cotangent,
):
    shard, ctx, tp = sizes
    micros, rows = frames.shape[0], frames.shape[2]
    width = query_weight.shape[1]
    ctx_index = lax.axis_index("ctx")

    inputs = [frames[m, 0].astype(jnp.float32) for m in range(micros)]
    hats1 = [normalize(x) for x in inputs]
    normed1 = [(hat * norm1_gain + norm1_bias).astype(LOW) for hat, _ in hats1]
    bias = jnp.concatenate([query_bias, jnp.zeros_like(query_bias), value_bias])[:, None]
    ids = ctx_index ^ jnp.arange(ctx, dtype=jnp.int32)
    valid = [jnp.clip(lengths[m, 0] - rows * ids, 0, rows) for m in range(micros)]

    def own_part(weight, split):
        count = weight.shape[0] // split
        return lax.dynamic_slice_in_dim(weight, lax.rem(ctx_index, split) * count, count, 0)

    full_qkv, full_out, full_up, full_down, queries, pairs, all_attended, kept, inverses = opening(
        sizes,
        jnp.stack(valid),
        jnp.concatenate(normed1, axis=0).T,
        bias,
        jnp.concatenate([own_part(w, 4) for w in (query_weight, key_weight, value_weight)], axis=1),
        own_part(out_weight, 4),
        own_part(up_weight, 4),
        own_part(down_weight, 2),
    )
    tp_index = lax.axis_index("tp")
    own_out = lax.dynamic_index_in_dim(full_out, tp_index, 0, keepdims=False)
    attended = [lax.dynamic_index_in_dim(all_attended[m], tp_index, 0, keepdims=False) for m in range(micros)]
    mixed, hats2, normed2, hidden = [], [], [], []
    for m in range(micros):
        branch = sum(contract(all_attended[m, t], full_out[t], ((0,), (1,))) for t in range(tp))
        mixed.append(inputs[m] + branch + out_bias)
        hats2.append(normalize(mixed[m]))
        normed2.append((hats2[m][0] * norm2_gain + norm2_bias).astype(LOW))
        hidden.append(contract(normed2[m], full_up, ((1,), (0,))) + up_bias)
    active, hidden_grads, outputs, mixed_grads, branch_grads = [], [], [], [], []
    normed2_grads = []
    for m in range(micros):
        cdf = 0.5 * (1.0 + lax.erf(hidden[m] * math.sqrt(0.5)))
        pdf = jnp.exp(-0.5 * hidden[m] * hidden[m]) * (1.0 / math.sqrt(2.0 * math.pi))
        active.append((hidden[m] * cdf).astype(LOW))
        slope = cdf + hidden[m] * pdf
        hidden_grads.append((contract(cotangent[m, 0], full_down, ((1,), (0,))) * slope).astype(LOW))
        normed2_grads.append(low_sum(contract(hidden_grads[m], full_up, ((1,), (1,))), "tp", tp))
    for m in range(micros):
        branch = low_sum(contract(active[m], full_down, ((1,), (1,))), "tp", tp)
        outputs.append((mixed[m] + branch + down_bias).astype(LOW))
        hat, inverse = hats2[m]
        mixed_grads.append(
            cotangent[m, 0].astype(jnp.float32) + normalize_grad(normed2_grads[m] * norm2_gain, hat, inverse)
        )
        branch_grads.append(mixed_grads[m].astype(LOW))
    projected_grads, normed1_terms, input_grads = [], [], []

    def finish_pairs(query_grad, chip):
        pair_grad = (chip[0].astype(jnp.float32) + swap(chip[1], "ctx", 2, ctx).astype(jnp.float32)).astype(LOW)
        return jnp.concatenate([query_grad, pair_grad.reshape(2 * width, rows)], axis=0)

    for m in range(micros):
        attended_grad = contract(own_out, branch_grads[m], ((0,), (1,))).astype(LOW)
        if m > 0:
            attended_grad, chip = lax.optimization_barrier((attended_grad, chip))
            projected_grads.append(finish_pairs(query_grad, chip))
        query_grad, pairs_grad = attention_backward(
            m, tp_index[None], queries, attended_grad, all_attended, inverses, kept, pairs
        )
        chip = (
            pairs_grad[: ctx // 2].astype(jnp.float32) + swap(pairs_grad[ctx // 2 :], "ctx", 1, ctx).astype(jnp.float32)
        ).astype(LOW)
    projected_grads.append(finish_pairs(query_grad, chip))
    for m in range(micros):
        normed1_terms.append(contract(projected_grads[m], full_qkv, ((0,), (1,))))
    gain1, bias1, normed1_grads = [], [], []
    for m in range(micros):
        hat, inverse = hats1[m]
        gain1.append(jnp.sum(normed1_terms[m] * hat, axis=0))
        bias1.append(jnp.sum(normed1_terms[m], axis=0))
        normed1_grads.append(low_sum_start(normed1_terms[m], "tp", tp))

    def over(items, dim):
        return jnp.concatenate(items, axis=dim)

    def row_sum(items):
        return sum(jnp.sum(item.astype(jnp.float32), axis=0) for item in items)

    small = jnp.concatenate(
        [
            sum(jnp.sum(g[:width].astype(jnp.float32), axis=1) for g in projected_grads),
            sum(jnp.sum(g[2 * width :].astype(jnp.float32), axis=1) for g in projected_grads),
            row_sum(hidden_grads),
            row_sum(mixed_grads),
            row_sum([normed2_grads[m] * hats2[m][0] for m in range(micros)]),
            row_sum(normed2_grads),
            row_sum([cotangent[m, 0] for m in range(micros)]),
        ]
    )
    first = jnp.concatenate([sum(gain1), sum(bias1)])
    blocks, small_sum, first_sum = closing(
        sizes,
        (False, False, True, True),
        as_tiles(small),
        as_tiles(first),
        (
            weight_terms(normed1, projected_grads, 0, ctx),
            weight_terms(branch_grads, attended, 0, ctx),
            weight_terms([over(normed2, 0)], [over(hidden_grads, 0)], 1, ctx),
            weight_terms([over([cotangent[m, 0] for m in range(micros)], 0)], [over(active, 0)], 1, ctx),
        ),
    )
    mine, blocks = lax.optimization_barrier(([total for total, _ in normed1_grads], blocks))
    normed1_grads = [a.astype(jnp.float32) + b[1].astype(jnp.float32) for a, b in zip(mine, normed1_grads)]
    for m in range(micros):
        hat, inverse = hats1[m]
        input_grads.append(mixed_grads[m] + normalize_grad(normed1_grads[m] * norm1_gain, hat, inverse))
    qkv_grad, out_grad, up_grad, down_grad = [whole_rows(b) for b in blocks]
    small = jnp.concatenate([small_sum.reshape(-1)[: small.shape[0]], first_sum.reshape(-1)[: first.shape[0]]])
    model = norm1_gain.shape[0]
    cuts, at = [], 0
    for count in (width, width, up_bias.shape[0], model, model, model, model, model, model):
        cuts.append(small[at : at + count])
        at += count
    query_bias_sum, value_bias_sum, up_bias_sum, out_bias_sum, gain2_sum, bias2_sum, down_bias_sum, gain1_sum, bias1_sum = cuts
    return (
        jnp.stack(outputs)[:, None],
        jnp.stack(input_grads)[:, None],
        gain1_sum,
        bias1_sum,
        qkv_grad[:, :width],
        query_bias_sum,
        qkv_grad[:, width : 2 * width],
        qkv_grad[:, 2 * width :],
        value_bias_sum,
        out_grad,
        out_bias_sum,
        gain2_sum,
        bias2_sum,
        up_grad,
        up_bias_sum,
        down_grad,
        down_bias_sum,
    )


def solution(mesh):
    sizes = (mesh.shape["shard"], mesh.shape["ctx"], mesh.shape["tp"])
    rows, weight, hidden, copied = P(None, "shard", "ctx", None), P("shard", "tp"), P("tp"), P()
    return jax.shard_map(
        functools.partial(body, sizes),
        mesh=mesh,
        in_specs=(
            rows,
            P(None, "shard"),
            copied,
            copied,
            weight,
            hidden,
            weight,
            weight,
            hidden,
            weight,
            copied,
            copied,
            copied,
            weight,
            hidden,
            weight,
            copied,
            rows,
        ),
        out_specs=(
            rows,
            rows,
            copied,
            copied,
            weight,
            hidden,
            weight,
            weight,
            hidden,
            weight,
            copied,
            copied,
            copied,
            weight,
            hidden,
            weight,
            copied,
        ),
        check_vma=False,
    )
```

```python
import functools
import math

import jax
import jax.numpy as jnp
from jax import lax
from jax.experimental import pallas as pl
from jax.experimental.pallas import tpu as pltpu
from jax.sharding import PartitionSpec as P

HEAD_DIM = 80
STEP = 512
SUB = 256
EPSILON = 1e-05
SCALE = HEAD_DIM**-0.5
LOW = jnp.bfloat16


def contract(left, right, dims):
    return lax.dot_general(left, right, (dims, ((), ())), preferred_element_type=jnp.float32)

class Weight:
    def __init__(self, index, piece, full, shard, split, ctx_index):
        self.index, self.piece, self.full, self.split = index, piece, full, split
        self.each = full.shape[-2] // shard
        self.rows = self.each // split
        self.part = lax.rem(ctx_index, split)

    def slice(self, shard_index, part):
        rows = pl.ds(pl.multiple_of(shard_index * self.each + part * self.rows, 16), self.rows)
        return self.full.at[:, rows] if len(self.full.shape) == 3 else self.full.at[rows]


def flip(index, bit):
    return index + bit - 2 * bit * lax.rem(index // bit, 2)


def opening_kernel(
    sizes,
    valid_ref,
    normed_ref,
    bias_ref,
    qkv_ref,
    out_ref,
    up_ref,
    down_ref,
    full_qkv,
    full_out,
    full_up,
    full_down,
    q_ref,
    kv_ref,
    a_ref,
    e_ref,
    inverse_ref,
    weights_ref,
    pairs_ref,
    mine_ref,
    s_ref,
    low_ref,
    z_send,
    z_recv,
    x_send,
    x_recv,
    c_send,
    c_recv,
    y_send,
    y_recv,
    kv_send,
    kv_recv,
    a_send,
    a_recv,
    own_sem,
    e_sem,
    last_sem,
):
    shard, ctx, tp = sizes
    width, rows = q_ref.shape[1], q_ref.shape[2]
    heads = width // HEAD_DIM
    i, p, me = lax.axis_index("shard"), lax.axis_index("ctx"), lax.axis_index("tp")
    across, beside = flip(p, 2), flip(p, 1)

    def remote(source, target, send, recv, **device):
        return pltpu.make_async_remote_copy(
            src_ref=source, dst_ref=target, send_sem=send, recv_sem=recv,
            device_id=device, device_id_type=pl.DeviceIdType.MESH,
        )

    def others():
        return [lax.rem(me + d, tp) for d in range(1, tp)]

    barrier = pltpu.get_barrier_semaphore()

    def greet(**device):
        pl.semaphore_signal(barrier, inc=1, device_id=device, device_id_type=pl.DeviceIdType.MESH)

    pl.when(i > 0)(lambda: greet(shard=i - 1))
    pl.when(i < shard - 1)(lambda: greet(shard=i + 1))
    greet(ctx=across)
    greet(ctx=beside)
    for other in others():
        greet(tp=other)
    pl.semaphore_wait(barrier, 2 + (tp - 1) + jnp.where(i > 0, 1, 0) + jnp.where(i < shard - 1, 1, 0))

    qkv = Weight(0, qkv_ref, weights_ref, shard, 4, p)
    out = Weight(1, out_ref, full_out, shard, 4, p)
    up = Weight(2, up_ref, full_up, shard, 4, p)
    down = Weight(3, down_ref, full_down, shard, 2, p)
    everything = (qkv, out, up, down)

    def z_copy(w, j, way):
        there = w.slice(j, w.part)
        return remote(there, there, z_send.at[w.index, (way + 1) // 2, j], z_recv.at[w.index, j], shard=i + way)

    def x_copy(w, j):
        there = w.slice(j, w.part)
        return remote(there, there, x_send.at[w.index, j], x_recv.at[w.index, j], ctx=across)

    def c_copy(w, j, which):
        there = w.slice(j, flip(w.part, 2) if which else w.part)
        return remote(there, there, c_send.at[w.index, j, which], c_recv.at[w.index, j, which], ctx=beside)

    def x_arriving(w, j):
        there = w.slice(j, flip(w.part, 2))
        return remote(there, there, x_send.at[w.index, j], x_recv.at[w.index, j], ctx=across)

    def c_arriving(w, j, which):
        there = w.slice(j, flip(flip(w.part, 2) if which else w.part, 1))
        return remote(there, there, c_send.at[w.index, j, which], c_recv.at[w.index, j, which], ctx=beside)

    def share(w, j):
        if w.split == 4 and w is not up:
            x_copy(w, j).start()
        c_copy(w, j, 0).start()

    def push(w):
        def one(j, carry):
            x_copy(w, j).start()
            return carry

        lax.fori_loop(0, shard, one, 0)

    def begin(w):
        pl.when(i < shard - 1)(lambda: z_copy(w, i, 1).start())
        pl.when(i > 0)(lambda: z_copy(w, i, -1).start())
        share(w, i)

    def arrive(w, hop):
        for way, there, j in ((1, i >= hop, i - hop), (-1, i + hop < shard, i + hop)):

            @pl.when(there)
            def _():
                z_copy(w, j, way).wait_recv()
                onward = (i < shard - 1) if way == 1 else (i > 0)
                pl.when(onward)(lambda: z_copy(w, j, way).start())
                share(w, j)

    def cross(w):
        def one(j, carry):
            x_arriving(w, j).wait_recv()
            c_copy(w, j, 1).start()
            return carry

        if w.split == 4:
            lax.fori_loop(0, shard, one, 0)

    def settle(w):
        def one(j, carry):
            c_arriving(w, j, 0).wait_recv()
            if w.split == 4:
                c_arriving(w, j, 1).wait_recv()
            return carry

        lax.fori_loop(0, shard, one, 0)

    def drain(w):
        def one(j, carry):
            pl.when((j <= i) & (i < shard - 1))(lambda: z_copy(w, j, 1).wait_send())
            pl.when((j >= i) & (i > 0))(lambda: z_copy(w, j, -1).wait_send())
            c_copy(w, j, 0).wait_send()
            if w.split == 4:
                x_copy(w, j).wait_send()
                c_copy(w, j, 1).wait_send()
            return carry

        lax.fori_loop(0, shard, one, 0)

    def own_copy(w):
        target = w.slice(i, w.part)
        if w is out:
            target = target.at[me]
        return pltpu.make_async_copy(w.piece, target, own_sem.at[w.index])

    for w in everything:
        own_copy(w).start()
    own_copy(qkv).wait()
    begin(qkv)

    def y_copy(source_me, other, slot):
        there = out.slice(i, out.part).at[source_me]
        return remote(there, there, y_send.at[slot], y_recv.at[slot], tp=other)

    own_copy(out).wait()
    for d in range(1, tp):
        y_copy(me, lax.rem(me + d, tp), d).start()
    own_copy(up).wait()
    own_copy(down).wait()
    for hop in range(1, shard):
        if hop == shard - 1:
            for d in range(1, tp):
                y_copy(lax.rem(me + tp - d, tp), lax.rem(me + tp - d, tp), d).wait_recv()
            begin(out)
        arrive(qkv, hop)
    cross(qkv)
    settle(qkv)
    keep_qkv = pltpu.make_async_copy(weights_ref, full_qkv, last_sem.at[0])
    keep_qkv.start()

    def project(m):
        columns = slice(m * rows, (m + 1) * rows)
        for which in range(3):
            for low in range(0, width, 256):
                high = min(width, low + 256)
                picked = slice(which * width + low, which * width + high)
                value = contract(weights_ref[:, picked], normed_ref[:, columns], ((0,), (0,))) + bias_ref[picked, 0:1]
                if which == 0:
                    q_ref[m, low:high] = (value * (SCALE * math.log2(math.e))).astype(LOW)
                else:
                    pairs_ref[m, 0, (which - 1) * width + low : (which - 1) * width + high] = value.astype(LOW)

    def kv_copy(m, source, target, to):
        return remote(
            pairs_ref.at[m, source], pairs_ref.at[m, target], kv_send.at[m, target - 1], kv_recv.at[m, target - 1], ctx=to
        )

    def send_pair(m):
        kv_copy(m, 0, 2, across).start()
        kv_copy(m, 0, 1, beside).start()

    def take_pair(m):
        kv_copy(m, 0, 2, across).wait_recv()
        kv_copy(m, 2, 3, beside).start()
        kv_copy(m, 0, 1, beside).wait_recv()
        kv_copy(m, 2, 3, beside).wait_recv()

    def e_copy(m, h):
        slot = lax.rem(h, 2)
        return pltpu.make_async_copy(low_ref.at[slot], e_ref.at[m, h], e_sem.at[slot])

    def attend(m, first, last):
        def one(h, carry):
            lanes = pl.ds(pl.multiple_of(h * HEAD_DIM, 16), HEAD_DIM)
            values = pl.ds(pl.multiple_of(width + h * HEAD_DIM, 16), HEAD_DIM)
            slot = lax.rem(h, 2)
            if m > 0:
                e_copy(m, h).wait()
            else:
                pl.when(h >= 2)(lambda: e_copy(m, h).wait())
            q = q_ref[m, lanes]
            top = jnp.full((1, rows), -1e30, jnp.float32)
            for b in range(ctx):
                s = contract(pairs_ref[m, b, lanes], q, ((0,), (0,)))
                at = lax.broadcasted_iota(jnp.int32, (rows, 1), 0)
                s = jnp.where(at < valid_ref[m, b], s, -1e30)
                s_ref[b] = s
                top = jnp.maximum(top, jnp.max(s, axis=0, keepdims=True))
            norm = jnp.zeros((1, rows), jnp.float32)
            total = jnp.zeros((HEAD_DIM, rows), jnp.float32)
            for b in range(ctx):
                e = jnp.exp2(s_ref[b] - top)
                norm = norm + jnp.sum(e, axis=0, keepdims=True)
                low = e.astype(LOW)
                low_ref[slot, b * rows : (b + 1) * rows] = low
                total = total + contract(pairs_ref[m, b, values], low, ((1,), (0,)))
            inverse = 1.0 / norm
            mine_ref[m, lanes] = (total * inverse).astype(LOW)
            inverse_ref[m, h] = jnp.broadcast_to(inverse, (8, rows))
            e_copy(m, h).start()
            return carry

        lax.fori_loop(first, last, one, 0)

    def a_copy(m, slot, other):
        return remote(mine_ref.at[m], a_ref.at[m, me], a_send.at[m, slot], a_recv.at[m, slot], tp=other)

    def a_arriving(m, slot, other):
        return remote(mine_ref.at[m], a_ref.at[m, other], a_send.at[m, slot], a_recv.at[m, slot], tp=other)

    def send_attended(m):
        for d in range(1, tp):
            a_copy(m, d, lax.rem(me + d, tp)).start()
        pltpu.make_async_copy(mine_ref.at[m], a_ref.at[m, me], last_sem.at[1 + m]).start()

    half = heads // 2
    project(0)
    send_pair(0)
    project(1)
    for hop in range(1, shard):
        if hop == shard - 1:
            begin(up)
        arrive(out, hop)
    for hop in range(1, shard - 1):
        arrive(up, hop)
    begin(down)
    cross(out)
    take_pair(0)
    send_pair(1)
    arrive(up, shard - 1)
    push(up)
    attend(0, 0, half)
    arrive(down, 1)
    attend(0, half, heads)
    send_attended(0)
    keep_pairs = [pltpu.make_async_copy(pairs_ref.at[m], kv_ref.at[m], last_sem.at[3 + m]) for m in range(2)]
    keep_pairs[0].start()
    for hop in range(2, shard - 1):
        arrive(down, hop)
    take_pair(1)
    attend(1, 0, heads)
    send_attended(1)
    keep_pairs[1].start()
    cross(up)
    arrive(down, shard - 1)
    settle(out)
    settle(up)
    settle(down)
    for w in everything:
        drain(w)
    for d in range(1, tp):
        y_copy(me, lax.rem(me + d, tp), d).wait_send()
    for m in range(2):
        kv_copy(m, 0, 2, across).wait_send()
        kv_copy(m, 0, 1, beside).wait_send()
        kv_copy(m, 2, 3, beside).wait_send()
        for d in range(1, tp):
            a_arriving(m, d, lax.rem(me + tp - d, tp)).wait_recv()
            a_copy(m, d, lax.rem(me + d, tp)).wait_send()
        pltpu.make_async_copy(mine_ref.at[m], a_ref.at[m, me], last_sem.at[1 + m]).wait()
        keep_pairs[m].wait()
    keep_qkv.wait()
    for h in (heads - 2, heads - 1):
        e_copy(1, h).wait()


def opening(sizes, valid, normed, bias, qkv, out, up, down):
    shard, ctx, tp = sizes
    width = qkv.shape[1] // 3
    model = qkv.shape[0] * 4 * shard
    rows = normed.shape[1] // 2
    heads = width // HEAD_DIM
    low = lambda *shape: jax.ShapeDtypeStruct(shape, LOW)
    anywhere, vmem = pl.BlockSpec(memory_space=pl.ANY), pl.BlockSpec(memory_space=pltpu.VMEM)
    dma = pltpu.SemaphoreType.DMA
    keys = ctx * rows
    return pl.pallas_call(
        functools.partial(opening_kernel, sizes),
        in_specs=[pl.BlockSpec(memory_space=pltpu.SMEM)] + [vmem] * 6,
        out_specs=[anywhere] * 4 + [vmem, anywhere, anywhere, anywhere, vmem],
        out_shape=[
            low(model, 3 * width),
            low(tp, model, width),
            low(model, up.shape[1]),
            low(model, down.shape[1]),
            low(2, width, rows),
            low(2, ctx, 2 * width, rows),
            low(2, tp, width, rows),
            low(2, heads, keys, rows),
            jax.ShapeDtypeStruct((2, heads, 8, rows), jnp.float32),
        ],
        scratch_shapes=[
            pltpu.VMEM((model, 3 * width), LOW),
            pltpu.VMEM((2, ctx, 2 * width, rows), LOW),
            pltpu.VMEM((2, width, rows), LOW),
            pltpu.VMEM((ctx, rows, rows), jnp.float32),
            pltpu.VMEM((2, keys, rows), LOW),
            dma((4, 2, shard)),
            dma((4, shard)),
            dma((4, shard)),
            dma((4, shard)),
            dma((4, shard, 2)),
            dma((4, shard, 2)),
            dma((tp,)),
            dma((tp,)),
            dma((2, 3)),
            dma((2, 3)),
            dma((2, tp)),
            dma((2, tp)),
            dma((4,)),
            dma((2,)),
            dma((5,)),
        ],
        compiler_params=pltpu.CompilerParams(collective_id=0, has_side_effects=True, vmem_limit_bytes=56 << 20),
        cost_estimate=pl.CostEstimate(
            flops=8 * heads * rows * keys * 256, bytes_accessed=80 << 20, transcendentals=2 * heads * rows * keys
        ),
        name="opening",
    )(valid, normed, bias, qkv, out, up, down)


def backward_kernel(q_ref, g_ref, a_ref, inverse_ref, e_ref, pairs_ref, dq_ref, pairs_grad_ref, acc_ref):
    ctx, rows = pairs_ref.shape[1], pairs_ref.shape[4]
    q = q_ref[0]
    g32 = g_ref[...].astype(jnp.float32) * inverse_ref[0, 0, 0:1]
    delta = jnp.sum(g32 * a_ref[0, 0].astype(jnp.float32), axis=0, keepdims=True)
    g = g32.astype(LOW)
    sub = min(SUB, rows)
    acc_ref[...] = jnp.zeros(acc_ref.shape, jnp.float32)
    for b in range(ctx):
        to = (b % 2) * 2 + b // 2
        parts = [(slice(o, o + sub), slice(b * rows + o, b * rows + o + sub)) for o in range(0, rows, sub)]
        grads = [contract(pairs_ref[0, b, 1, :, c], g, ((0,), (0,))) for c, _ in parts]
        total = None
        for (c, r), grad in zip(parts, grads):
            e = e_ref[0, 0, r]
            pairs_grad_ref[to, 1, :, c] = contract(g, e, ((1,), (1,))).astype(LOW)
            ds = (e.astype(jnp.float32) * (grad - delta)).astype(LOW)
            term = contract(pairs_ref[0, b, 0, :, c], ds, ((1,), (0,)))
            total = term if total is None else total + term
            pairs_grad_ref[to, 0, :, c] = (contract(q, ds, ((1,), (1,))) * math.log(2.0)).astype(LOW)
        acc_ref[...] += total
    dq_ref[...] = (acc_ref[...] * SCALE).astype(LOW)


def attention_backward(micro, own, queries, grad, attended, inverses, kept, pairs):
    _, width, rows = queries.shape
    heads, ctx = width // HEAD_DIM, pairs.shape[1]
    keys = ctx * rows
    pairs = pairs.reshape(pairs.shape[0], ctx, 2, width, rows)
    grid = pltpu.PrefetchScalarGridSpec(
        num_scalar_prefetch=1,
        grid=(heads,),
        in_specs=[
            pl.BlockSpec((1, HEAD_DIM, rows), lambda h, own: (micro, h, 0)),
            pl.BlockSpec((HEAD_DIM, rows), lambda h, own: (h, 0)),
            pl.BlockSpec((1, 1, HEAD_DIM, rows), lambda h, own: (micro, own[0], h, 0)),
            pl.BlockSpec((1, 1, 8, rows), lambda h, own: (micro, h, 0, 0)),
            pl.BlockSpec((1, 1, keys, rows), lambda h, own: (micro, h, 0, 0)),
            pl.BlockSpec((1, ctx, 2, HEAD_DIM, rows), lambda h, own: (micro, 0, 0, h, 0)),
        ],
        out_specs=[
            pl.BlockSpec((HEAD_DIM, rows), lambda h, own: (h, 0)),
            pl.BlockSpec((ctx, 2, HEAD_DIM, rows), lambda h, own: (0, 0, h, 0)),
        ],
        scratch_shapes=[pltpu.VMEM((HEAD_DIM, rows), jnp.float32)],
    )
    return pl.pallas_call(
        lambda own_ref, *refs: backward_kernel(*refs),
        grid_spec=grid,
        out_shape=[
            jax.ShapeDtypeStruct((width, rows), LOW),
            jax.ShapeDtypeStruct((ctx, 2, width, rows), LOW),
        ],
        compiler_params=pltpu.CompilerParams(vmem_limit_bytes=40 << 20),
        cost_estimate=pl.CostEstimate(
            flops=8 * rows * keys * 256 * heads, bytes_accessed=heads * keys * rows * 2, transcendentals=0
        ),
        name="attention_backward",
    )(own, queries, grad, attended, inverses, kept, pairs)


def swap(value, axis, bit, size):
    return lax.ppermute(value, axis, [(k, k ^ bit) for k in range(size)])


def bits_of(size):
    found, bit = [], size // 2
    while bit > 0:
        found.append(bit)
        bit //= 2
    return found


def low_sum_start(value, axis, size):
    total = value.astype(LOW)
    if size == 1:
        return total, jnp.zeros_like(total)
    for bit in reversed(bits_of(size)):
        got = swap(total, axis, bit, size)
        if bit == size // 2:
            return total, got
        total = (total.astype(jnp.float32) + got.astype(jnp.float32)).astype(LOW)


def low_sum(value, axis, size):
    total, got = low_sum_start(value, axis, size)
    return (total.astype(jnp.float32) + got.astype(jnp.float32)).astype(LOW).astype(jnp.float32)


class Gradient:
    def __init__(self, index, across_first, terms, refs):
        self.index, self.across_first, self.terms = index, across_first, terms
        self.result, self.near, self.far, self.hops, self.crossed = refs
        self.sums = (self.near, self.far)
        self.halves = (0,) if across_first else (0, 1)


def closing_kernel(sizes, across_first, normed_ref, projected_ref, small_ref, first_ref, *refs):
    shard, ctx, tp = sizes
    units = len(across_first)
    given, refs = refs[: 4 * units - 4], refs[4 * units - 4 :]
    results, refs = refs[:units], refs[units:]
    small_out, first_out, refs = refs[0], refs[1], refs[2:]
    scratch, refs = refs[: 4 * units], refs[4 * units :]
    product_near, product_far, refs = refs[0], refs[1], refs[2:]
    terms = (None, product_near, None, product_far) + tuple(given)
    small_got, first_got, c_send, c_recv, x_send, x_recv, z_send, z_recv, g_send, g_recv, v_send, v_recv = refs
    i, p, me = lax.axis_index("shard"), lax.axis_index("ctx"), lax.axis_index("tp")
    across, beside = flip(p, 2), flip(p, 1)
    grads = [
        Gradient(u, across_first[u], terms[4 * u : 4 * u + 4], (results[u],) + tuple(scratch[4 * u : 4 * u + 4]))
        for u in range(units)
    ]

    def remote(source, target, send, recv, **device):
        return pltpu.make_async_remote_copy(
            src_ref=source, dst_ref=target, send_sem=send, recv_sem=recv,
            device_id=device, device_id_type=pl.DeviceIdType.MESH,
        )

    barrier = pltpu.get_barrier_semaphore()

    def greet(**device):
        pl.semaphore_signal(barrier, inc=1, device_id=device, device_id_type=pl.DeviceIdType.MESH)

    partners = [("tp", me, bit) for bit in reversed(bits_of(tp))]
    partners += [("ctx", p, bit) for bit in reversed(bits_of(ctx))]
    partners += [("shard", i, bit) for bit in reversed(bits_of(shard))]
    for axis, index, bit in partners:
        greet(**{axis: flip(index, bit)})
    skipped = jnp.where(i > 0, jnp.where(lax.rem(i, 2) == 0, 1, 0), 0)
    ahead = jnp.where(i < shard - 1, jnp.where(lax.rem(i, 2) == 1, 1, 0), 0)
    pl.when(skipped == 1)(lambda: greet(shard=i - 1))
    pl.when(ahead == 1)(lambda: greet(shard=i + 1))
    pl.semaphore_wait(barrier, len(partners) + skipped + ahead)

    def rows_of(ref, j):
        each = ref.shape[-2] // shard
        return ref.at[pl.ds(pl.multiple_of(j * each, 16), each)]

    def c_copy(g, j, which):
        source = g.terms[3 if which else 1]
        target = g.far if which else g.near
        return remote(
            rows_of(source, j), rows_of(target, j),
            c_send.at[g.index, j, which], c_recv.at[g.index, j, which], ctx=beside,
        )

    def x_copy(g, j):
        return remote(
            rows_of(g.sums[1], j), rows_of(g.crossed, j), x_send.at[g.index, j], x_recv.at[g.index, j], ctx=across
        )

    def z_copy(g, half, way, step, j):
        return remote(
            rows_of(g.sums[half], j), g.hops.at[half, way, step],
            z_send.at[g.index, half, way, step], z_recv.at[g.index, half, way, step], shard=i + 1 - 2 * way,
        )

    def add_to(target, value):
        target[...] = (target[...].astype(jnp.float32) + value.astype(jnp.float32)).astype(LOW)

    def every_shard(one):
        lax.fori_loop(0, shard, lambda j, carry: (one(j), carry)[1], 0)

    def send_near(g):
        def one(j):
            c_copy(g, j, 0).start()
            c_copy(g, j, 1).start()

        every_shard(one)

    def product(owner, store):
        count = projected_ref.shape[1] // ctx
        rows = pl.ds(pl.multiple_of(owner * count, math.gcd(count, 16)), count)
        model = normed_ref.shape[2]
        for low in range(0, model, 256):
            cols = slice(low, min(model, low + 256))
            total = 0.0
            for m in range(2):
                total = total + contract(projected_ref[m, rows], normed_ref[m, :, cols], ((1,), (0,)))
            store(cols, total.T)

    def put(target):
        def store(cols, value):
            target[cols] = value.astype(LOW)

        return store

    def add(target):
        def store(cols, value):
            target[cols] = (target[cols].astype(jnp.float32) + value).astype(LOW)

        return store

    def meet(g, j):
        c_copy(g, j, 0).wait_recv()
        c_copy(g, j, 1).wait_recv()
        for half, got in ((0, g.near), (1, g.far)):
            add_to(rows_of(got, j), rows_of(g.terms[2 * half], j)[...])
        if g.across_first:
            x_copy(g, j).start()

    def joined(g, j):
        x_copy(g, j).wait_recv()
        add_to(rows_of(g.sums[0], j), rows_of(g.crossed, j)[...])

    def hop(g, step):
        for half in g.halves:
            for way, at in ((0, i), (1, shard - 1 - i)):
                j = shard - 1 - step + at if way == 0 else step - at

                @pl.when((at <= step) & (at < shard - 1))
                def _():
                    @pl.when(at > 0)
                    def _():
                        z_copy(g, half, way, step - 1, j).wait_recv()
                        add_to(rows_of(g.sums[half], j), g.hops[half, way, step - 1])

                    z_copy(g, half, way, step, j).start()

    def arrive(g):
        for half in g.halves:
            for way, at in ((0, i), (1, shard - 1 - i)):

                @pl.when(at > 0)
                def _():
                    z_copy(g, half, way, shard - 2, i).wait_recv()
                    add_to(rows_of(g.sums[half], i), g.hops[half, way, shard - 2])

    def side_copy(g):
        return remote(rows_of(g.sums[1], i), g.crossed, x_send.at[g.index, 0], x_recv.at[g.index, 0], ctx=across)

    def spread_copy(g, which):
        owner = across if which == 2 else p
        to = across if which == 0 else beside
        return remote(
            g.result.at[owner], g.result.at[owner], g_send.at[g.index, which], g_recv.at[g.index, which], ctx=to
        )

    def spread_arriving(g, which):
        owner = (across, beside, flip(across, 1))[which]
        to = across if which == 0 else beside
        return remote(
            g.result.at[owner], g.result.at[owner], g_send.at[g.index, which], g_recv.at[g.index, which], ctx=to
        )

    def finish(g):
        g.result[p] = rows_of(g.sums[0], i)[...]
        spread_copy(g, 0).start()
        spread_copy(g, 1).start()

    vectors = ((0, small_ref, small_out, small_got), (1, first_ref, first_out, first_got))

    def v_copy(number, which):
        axis, index, bit = partners[number]
        _, _, total, got = vectors[which]
        return remote(
            total.at[number], got.at[number], v_send.at[number, which], v_recv.at[number, which], **{axis: flip(index, bit)}
        )

    def meant(number):
        return (1,) if partners[number][0] == "tp" else (0, 1)

    def vector_start(number):
        for which in meant(number):
            v_copy(number, which).start()

    def vector_take(number):
        for which, _, total, got in vectors:
            if which in meant(number):
                v_copy(number, which).wait_recv()
                total[number + 1] = total[number] + got[number]
            else:
                total[number + 1] = total[number]

    small_out[0] = small_ref[...]
    first_out[0] = first_ref[...]
    vector_start(0)
    qkv, out, up, down = grads
    for g in (down, up, out):
        send_near(g)
    every_shard(lambda j: meet(down, j))
    hop(down, 0)
    every_shard(lambda j: meet(up, j))
    product(beside, put(product_near))
    product(flip(across, 1), put(product_far))
    send_near(qkv)
    every_shard(lambda j: meet(out, j))
    hop(down, 1)
    number = 0

    def next_vector():
        nonlocal number
        if number < len(partners):
            vector_take(number)
            number += 1
            if number < len(partners):
                vector_start(number)

    def met(j):
        c_copy(qkv, j, 0).wait_recv()
        c_copy(qkv, j, 1).wait_recv()

    every_shard(met)
    product(across, add(qkv.far))
    every_shard(lambda j: x_copy(qkv, j).start())
    product(p, add(qkv.near))
    for step in range(2, shard - 1):
        hop(down, step)
    next_vector()
    every_shard(lambda j: joined(up, j))
    hop(up, 0)
    next_vector()
    arrive(down)
    side_copy(down).start()
    every_shard(lambda j: joined(out, j))
    hop(out, 0)
    hop(up, 1)
    next_vector()
    every_shard(lambda j: joined(qkv, j))
    hop(qkv, 0)
    hop(out, 1)
    next_vector()
    side_copy(down).wait_recv()
    add_to(rows_of(down.sums[0], i), down.crossed[...])
    finish(down)
    for step in range(2, shard - 1):
        hop(up, step)
    hop(qkv, 1)
    arrive(up)
    finish(up)
    for step in range(2, shard - 1):
        hop(out, step)
        hop(qkv, step)
    arrive(out)
    finish(out)
    arrive(qkv)
    finish(qkv)
    while number < len(partners):
        next_vector()
    for g in grads:
        spread_arriving(g, 0).wait_recv()
        spread_copy(g, 2).start()
    for g in grads:
        spread_arriving(g, 1).wait_recv()
        spread_arriving(g, 2).wait_recv()
    for g in grads:

        def drain(j):
            c_copy(g, j, 0).wait_send()
            c_copy(g, j, 1).wait_send()
            if g.across_first:
                x_copy(g, j).wait_send()

        every_shard(drain)
        if not g.across_first:
            side_copy(g).wait_send()
        for half in g.halves:
            for way, at in ((0, i), (1, shard - 1 - i)):
                for step in range(shard - 1):
                    j = shard - 1 - step + at if way == 0 else step - at

                    @pl.when((at <= step) & (at < shard - 1))
                    def _():
                        z_copy(g, half, way, step, j).wait_send()

        for which in range(3):
            spread_copy(g, which).wait_send()
    for n in range(len(partners)):
        for which in meant(n):
            v_copy(n, which).wait_send()


def closing(sizes, across_first, normed, projected, small, first, terms):
    shard, ctx, tp = sizes
    units = len(across_first)
    vmem = pl.BlockSpec(memory_space=pltpu.VMEM)
    dma = pltpu.SemaphoreType.DMA
    stages = len(bits_of(tp)) + len(bits_of(ctx)) + len(bits_of(shard))
    shapes = [(normed.shape[2], projected.shape[1] // ctx)] + [t[0].shape for t in terms]
    scratch = []
    for (model, n), early in zip(shapes, across_first):
        each, halves = model // shard, 1 if early else 2
        scratch += [
            pltpu.VMEM((model, n), LOW),
            pltpu.VMEM((model, n), LOW),
            pltpu.VMEM((halves, 2, shard - 1, each, n), LOW),
            pltpu.VMEM((model, n) if early else (each, n), LOW),
        ]
    found = pl.pallas_call(
        functools.partial(closing_kernel, sizes, across_first),
        in_specs=[vmem] * (4 + 4 * units - 4),
        out_specs=[vmem] * (units + 2),
        out_shape=[jax.ShapeDtypeStruct((ctx, model // shard, n), LOW) for model, n in shapes]
        + [jax.ShapeDtypeStruct((stages + 1,) + v.shape, jnp.float32) for v in (small, first)],
        scratch_shapes=scratch
        + [pltpu.VMEM(shapes[0], LOW)] * 2
        + [pltpu.VMEM((stages,) + v.shape, jnp.float32) for v in (small, first)]
        + [
            dma((units, shard, 2)),
            dma((units, shard, 2)),
            dma((units, shard)),
            dma((units, shard)),
            dma((units, 2, 2, shard - 1)),
            dma((units, 2, 2, shard - 1)),
            dma((units, 3)),
            dma((units, 3)),
            dma((stages, 2)),
            dma((stages, 2)),
        ],
        compiler_params=pltpu.CompilerParams(collective_id=1, has_side_effects=True, vmem_limit_bytes=56 << 20),
        cost_estimate=pl.CostEstimate(flops=0, bytes_accessed=200 << 20, transcendentals=0),
        name="closing",
    )(normed, projected, small, first, *[t for four in terms for t in four])
    return found[:units], found[units][stages], found[units + 1][stages]


def weight_terms(lefts, rights, right_dim, ctx):
    count = rights[0].shape[right_dim] // ctx
    me = lax.axis_index("ctx")

    def term(mask):
        total = 0.0
        for left, right in zip(lefts, rights):
            part = lax.dynamic_slice_in_dim(right, (me ^ mask) * count, count, right_dim)
            total = total + contract(left, part, ((0,), (1 - right_dim,)))
        return total.astype(LOW)

    return [term(mask) for mask in range(ctx)]


def whole_rows(blocks):
    ctx, each, n = blocks.shape
    return jnp.moveaxis(blocks, 0, 1).reshape(each, ctx * n).astype(jnp.float32)


def as_tiles(vector):
    count = -(-vector.shape[0] // 1024) * 1024
    return jnp.pad(vector, (0, count - vector.shape[0])).reshape(-1, 128)


def normalize(values):
    center = values - jnp.mean(values, axis=-1, keepdims=True)
    spread_of = jnp.mean(center * center, axis=-1, keepdims=True)
    inverse = lax.rsqrt(spread_of + EPSILON)
    return center * inverse, inverse


def normalize_grad(grad, hat, inverse):
    return inverse * (
        grad - jnp.mean(grad, axis=-1, keepdims=True) - hat * jnp.mean(grad * hat, axis=-1, keepdims=True)
    )


def body(
    sizes,
    frames,
    lengths,
    norm1_gain,
    norm1_bias,
    query_weight,
    query_bias,
    key_weight,
    value_weight,
    value_bias,
    out_weight,
    out_bias,
    norm2_gain,
    norm2_bias,
    up_weight,
    up_bias,
    down_weight,
    down_bias,
    cotangent,
):
    shard, ctx, tp = sizes
    micros, rows = frames.shape[0], frames.shape[2]
    width = query_weight.shape[1]
    ctx_index = lax.axis_index("ctx")

    inputs = [frames[m, 0].astype(jnp.float32) for m in range(micros)]
    hats1 = [normalize(x) for x in inputs]
    normed1 = [(hat * norm1_gain + norm1_bias).astype(LOW) for hat, _ in hats1]
    bias = jnp.concatenate([query_bias, jnp.zeros_like(query_bias), value_bias])[:, None]
    ids = ctx_index ^ jnp.arange(ctx, dtype=jnp.int32)
    valid = [jnp.clip(lengths[m, 0] - rows * ids, 0, rows) for m in range(micros)]

    def own_part(weight, split):
        count = weight.shape[0] // split
        return lax.dynamic_slice_in_dim(weight, lax.rem(ctx_index, split) * count, count, 0)

    full_qkv, full_out, full_up, full_down, queries, pairs, all_attended, kept, inverses = opening(
        sizes,
        jnp.stack(valid),
        jnp.concatenate(normed1, axis=0).T,
        bias,
        jnp.concatenate([own_part(w, 4) for w in (query_weight, key_weight, value_weight)], axis=1),
        own_part(out_weight, 4),
        own_part(up_weight, 4),
        own_part(down_weight, 2),
    )
    tp_index = lax.axis_index("tp")
    own_out = lax.dynamic_index_in_dim(full_out, tp_index, 0, keepdims=False)
    attended = [lax.dynamic_index_in_dim(all_attended[m], tp_index, 0, keepdims=False) for m in range(micros)]
    mixed, hats2, normed2, hidden = [], [], [], []
    for m in range(micros):
        branch = sum(contract(all_attended[m, t], full_out[t], ((0,), (1,))) for t in range(tp))
        mixed.append(inputs[m] + branch + out_bias)
        hats2.append(normalize(mixed[m]))
        normed2.append((hats2[m][0] * norm2_gain + norm2_bias).astype(LOW))
        hidden.append(contract(normed2[m], full_up, ((1,), (0,))) + up_bias)
    active, hidden_grads, outputs, mixed_grads, branch_grads = [], [], [], [], []
    normed2_grads = []
    for m in range(micros):
        cdf = 0.5 * (1.0 + lax.erf(hidden[m] * math.sqrt(0.5)))
        pdf = jnp.exp(-0.5 * hidden[m] * hidden[m]) * (1.0 / math.sqrt(2.0 * math.pi))
        active.append((hidden[m] * cdf).astype(LOW))
        slope = cdf + hidden[m] * pdf
        hidden_grads.append((contract(cotangent[m, 0], full_down, ((1,), (0,))) * slope).astype(LOW))
        normed2_grads.append(low_sum_start(contract(hidden_grads[m], full_up, ((1,), (1,))), "tp", tp))

    def over(items, dim):
        return jnp.concatenate(items, axis=dim)

    up_terms = weight_terms([over(normed2, 0)], [over(hidden_grads, 0)], 1, ctx)
    mine, up_terms = lax.optimization_barrier(([total for total, _ in normed2_grads], up_terms))
    normed2_grads = [
        (a.astype(jnp.float32) + b[1].astype(jnp.float32)).astype(LOW).astype(jnp.float32)
        for a, b in zip(mine, normed2_grads)
    ]
    for m in range(micros):
        hat, inverse = hats2[m]
        mixed_grads.append(
            cotangent[m, 0].astype(jnp.float32) + normalize_grad(normed2_grads[m] * norm2_gain, hat, inverse)
        )
        branch_grads.append(mixed_grads[m].astype(LOW))
    projected_grads, normed1_terms, input_grads = [], [], []

    def finish_pairs(query_grad, chip):
        pair_grad = (chip[0].astype(jnp.float32) + swap(chip[1], "ctx", 2, ctx).astype(jnp.float32)).astype(LOW)
        return jnp.concatenate([query_grad, pair_grad.reshape(2 * width, rows)], axis=0)

    for m in range(micros):
        attended_grad = contract(own_out, branch_grads[m], ((0,), (1,))).astype(LOW)
        if m > 0:
            attended_grad, chip = lax.optimization_barrier((attended_grad, chip))
            projected_grads.append(finish_pairs(query_grad, chip))
        query_grad, pairs_grad = attention_backward(
            m, tp_index[None], queries, attended_grad, all_attended, inverses, kept, pairs
        )
        chip = (
            pairs_grad[: ctx // 2].astype(jnp.float32) + swap(pairs_grad[ctx // 2 :], "ctx", 1, ctx).astype(jnp.float32)
        ).astype(LOW)
        if m == 0:
            late, query_grad = lax.optimization_barrier((active, query_grad))
            branches = low_sum_start(contract(over(late, 0), full_down, ((1,), (1,))), "tp", tp)
    active, query_grad, projected_grads = lax.optimization_barrier((active, query_grad, projected_grads))
    down_terms = weight_terms([over([cotangent[m, 0] for m in range(micros)], 0)], [over(active, 0)], 1, ctx)
    projected_grads.append(finish_pairs(query_grad, chip))
    for m in range(micros):
        normed1_terms.append(contract(projected_grads[m], full_qkv, ((0,), (1,))))
    gain1, bias1, normed1_grads = [], [], []
    for m in range(micros):
        hat, inverse = hats1[m]
        gain1.append(jnp.sum(normed1_terms[m] * hat, axis=0))
        bias1.append(jnp.sum(normed1_terms[m], axis=0))
    normed1_grads = low_sum_start(over(normed1_terms, 0), "tp", tp)

    def row_sum(items):
        return sum(jnp.sum(item.astype(jnp.float32), axis=0) for item in items)

    small = jnp.concatenate(
        [
            sum(jnp.sum(g[:width].astype(jnp.float32), axis=1) for g in projected_grads),
            sum(jnp.sum(g[2 * width :].astype(jnp.float32), axis=1) for g in projected_grads),
            row_sum(hidden_grads),
            row_sum(mixed_grads),
            row_sum([normed2_grads[m] * hats2[m][0] for m in range(micros)]),
            row_sum(normed2_grads),
            row_sum([cotangent[m, 0] for m in range(micros)]),
        ]
    )
    first = jnp.concatenate([sum(gain1), sum(bias1)])
    blocks, small_sum, first_sum = closing(
        sizes,
        (True, True, True, False),
        jnp.stack(normed1),
        jnp.stack(projected_grads),
        as_tiles(small),
        as_tiles(first),
        (
            weight_terms(branch_grads, attended, 0, ctx),
            up_terms,
            down_terms,
        ),
    )
    mine, own_branch, blocks = lax.optimization_barrier((normed1_grads[0], branches[0], blocks))
    normed1_grads = (mine.astype(jnp.float32) + normed1_grads[1].astype(jnp.float32)).reshape(micros, rows, -1)
    branches = (own_branch.astype(jnp.float32) + branches[1].astype(jnp.float32)).astype(LOW).astype(jnp.float32)
    branches = branches.reshape(micros, rows, -1)
    for m in range(micros):
        outputs.append((mixed[m] + branches[m] + down_bias).astype(LOW))
    for m in range(micros):
        hat, inverse = hats1[m]
        input_grads.append(mixed_grads[m] + normalize_grad(normed1_grads[m] * norm1_gain, hat, inverse))
    qkv_grad, out_grad, up_grad, down_grad = [whole_rows(b) for b in blocks]
    small = jnp.concatenate([small_sum.reshape(-1)[: small.shape[0]], first_sum.reshape(-1)[: first.shape[0]]])
    model = norm1_gain.shape[0]
    cuts, at = [], 0
    for count in (width, width, up_bias.shape[0], model, model, model, model, model, model):
        cuts.append(small[at : at + count])
        at += count
    query_bias_sum, value_bias_sum, up_bias_sum, out_bias_sum, gain2_sum, bias2_sum, down_bias_sum, gain1_sum, bias1_sum = cuts
    return (
        jnp.stack(outputs)[:, None],
        jnp.stack(input_grads)[:, None],
        gain1_sum,
        bias1_sum,
        qkv_grad[:, :width],
        query_bias_sum,
        qkv_grad[:, width : 2 * width],
        qkv_grad[:, 2 * width :],
        value_bias_sum,
        out_grad,
        out_bias_sum,
        gain2_sum,
        bias2_sum,
        up_grad,
        up_bias_sum,
        down_grad,
        down_bias_sum,
    )


def solution(mesh):
    sizes = (mesh.shape["shard"], mesh.shape["ctx"], mesh.shape["tp"])
    rows, weight, hidden, copied = P(None, "shard", "ctx", None), P("shard", "tp"), P("tp"), P()
    return jax.shard_map(
        functools.partial(body, sizes),
        mesh=mesh,
        in_specs=(
            rows,
            P(None, "shard"),
            copied,
            copied,
            weight,
            hidden,
            weight,
            weight,
            hidden,
            weight,
            copied,
            copied,
            copied,
            weight,
            hidden,
            weight,
            copied,
            rows,
        ),
        out_specs=(
            rows,
            rows,
            copied,
            copied,
            weight,
            hidden,
            weight,
            weight,
            hidden,
            weight,
            copied,
            copied,
            copied,
            weight,
            hidden,
            weight,
            copied,
        ),
        check_vma=False,
    )
```
